256 devices in a mesh: member: 8 (over z_lo, core), shard: 32 (over x, y, z_hi).
Axes of the slice: x: 4, y: 4, z: 8 (z_hi: 2, z_lo: 4; z = z_hi * 4 + z_lo), core: 2. Of those that a mesh axis runs over, the one named last changes fastest.
Arguments:
- latent: bfloat16 [8, 1024, 1024], P('member', 'shard'), may hold values from -6 to 6
- grid_embed: bfloat16 [8192, 1024], P('shard'), may hold values from -6 to 6
- edge_src: int32 [8192, 3], P('shard'), may hold values from 0 to 1023, as said below
- area: float32 [8192], P('shard'), may hold values from 0.15 to 27
- target: float32 [8192, 100], P('shard'), may hold values from -6 to 6
- w_query: bfloat16 [1024, 1024], replicated, may hold values from -0.1875 to 0.1875
- w_keyval: bfloat16 [1024, 2048], replicated, may hold values from -0.1875 to 0.1875
- w_head: bfloat16 [1024, 100], replicated, may hold values from -0.1875 to 0.1875
Outputs:
- loss: float32 [8], P('member')
- d_latent: float32 [8, 1024, 1024], P('member', 'shard')
- grad_query: float32 [1024, 1024], P('shard')
- grad_keyval: float32 [1024, 2048], P('shard')
- grad_head: float32 [1024, 100], P('shard')
The draws below stay inside these ranges and needn't reach their ends.
Inputs may be any that keep to these rules, and one draw needn't show every extreme that they name: edge_src[g, k] is a node of the latent block of index g // 256 or of one of the two blocks beside it, cyclically, where block b holds nodes b * 32 to (b + 1) * 32 - 1.
All inputs are finite; a program needn't handle non-finite values.
Results may differ from the reference program's by a relative error of at most 0.035.
Values may be sent and summed in bfloat16 or wider, within the bound.
No kernel may reach another device: no remote copies, remote signals or barrier semaphores. Data moves between devices by JAX's collectives and lax.ppermute only.
A program may use at most 128 MiB of HBM per device.

```python
import math
import jax
import jax.numpy as jnp
from jax import lax

D = 1024
HEADS = 16
VARS = 100
KNB = 3
G_DEV = 256
H_DEV = 32
GN = 8192
HN = 1024
MEMBERS = 8
N_SHARD = 32


def draw_edge_src(key, part):
    key = jax.random.fold_in(key, 11)
    first, second = jax.random.split(key)
    owner = jnp.arange(GN, dtype=jnp.int32) // G_DEV
    offsets = jax.random.randint(first, (GN, KNB), -1, 2, dtype=jnp.int32)
    within = jax.random.randint(second, (GN, KNB), 0, H_DEV, dtype=jnp.int32)
    block = jnp.mod(owner[:, None] + offsets, N_SHARD)
    return (block * H_DEV + within).astype(jnp.int32)


def draw_area(key, part):
    key = jax.random.fold_in(key, 23)
    points = jnp.arange(GN, dtype=jnp.int32)
    across = (points // G_DEV).astype(jnp.float32) / (N_SHARD - 1)
    inside = (points % G_DEV).astype(jnp.float32) / G_DEV
    ramp = (1.0 + 2.0 * across) * (1.0 + 2.0 * inside)
    base = jnp.exp(jax.random.uniform(key, (GN,), jnp.float32, jnp.log(0.3), jnp.log(3.0)))
    return (base * ramp).astype(jnp.float32)


def raised(entries, rng, source, target, shards_of, factor):
    def block_of(dim):
        return (jnp.arange(entries.shape[dim]) // (entries.shape[dim] // shards_of)).reshape((-1,) + (1,) * (entries.ndim - 1 - dim))

    near = jax.random.permutation(rng, shards_of)[block_of(target)]
    far = (block_of(target) + shards_of // 2) % shards_of
    return jnp.where((block_of(source) == near) | (block_of(source) == far), factor * entries, entries)


def level_of(stream_key, extent, pieces, low, high):
    def one(dim, parts):
        steps = jax.random.uniform(jax.random.fold_in(jax.random.fold_in(stream_key, 6), dim), (parts,), jnp.float32, low / len(pieces), high / len(pieces))
        return jnp.repeat(jnp.exp(steps), extent[dim] // parts).reshape((-1,) + (1,) * (len(extent) - dim - 1))

    factor_of = one(*pieces[0])
    for cut in pieces[1:]:
        factor_of = factor_of * one(*cut)
    return factor_of


def noise(stream_key, shape, scale, reach, cuts=(), kind=jnp.bfloat16):
    gain = level_of(stream_key, shape, cuts, -0.22, 0.18) if cuts else 1.0
    drawn = jax.random.normal(stream_key, shape, jnp.float32) * scale * gain
    return jnp.minimum(jnp.maximum(drawn, -reach), reach).astype(kind)


def heavy_noise(stream_key, dims, deviation, reach, shards, heavy, kind=jnp.bfloat16):
    values = deviation * jax.random.normal(stream_key, dims, jnp.float32)
    if shards:
        values = values * level_of(stream_key, dims, shards, -0.22, 0.18)
    return jnp.clip(raised(values, jax.random.fold_in(stream_key, 3), *heavy), -reach, reach).astype(kind)


def setup_inputs(seed: int = 0) -> dict:
    streams_of = jax.random.split(jax.random.key(seed), 9)
    return {
        "latent": heavy_noise(streams_of[0], (MEMBERS, HN, D), 1.0, 6.0, ((0, 8), (1, 32)), (1, 2, 32, 2.75)),
        "grid_embed": heavy_noise(streams_of[1], (GN, D), 1.0, 6.0, ((0, 32),), (0, 1, 32, 2.75)),
        "edge_src": draw_edge_src(jax.random.fold_in(streams_of[8], 71), 0),
        "area": draw_area(jax.random.fold_in(streams_of[8], 71), 0),
        "target": noise(streams_of[4], (GN, VARS), 1.0, 6.0, ((0, 32),), jnp.float32),
        "w_query": noise(streams_of[5], (D, D), D ** -0.5, 0.1875),
        "w_keyval": noise(streams_of[6], (D, 2 * D), D ** -0.5, 0.1875),
        "w_head": noise(streams_of[7], (D, VARS), D ** -0.5, 0.1875),
    }


def normalize_heads(values):
    shaped = values.reshape(values.shape[:-1] + (HEADS, values.shape[-1] // HEADS))
    return shaped * lax.rsqrt(lax.optimization_barrier(jnp.mean(shaped * shaped, -1, keepdims=True)) + 1e-06)

def attend(query, table, source):
    width = query.shape[-1]
    size = width // HEADS
    picked = table[source]
    query_norm = normalize_heads(query)
    key_norm = normalize_heads(picked[..., :width])
    values = picked[..., width:].reshape(picked.shape[:2] + (HEADS, size))
    score = jnp.einsum('bhs,bkhs->bhk', query_norm, key_norm) * size ** (-0.5)
    expon = jnp.exp(score)
    weight = expon / lax.optimization_barrier(jnp.sum(expon, -1, keepdims=True))
    return jnp.einsum('bhk,bkhs->bhs', weight, values).reshape(query.shape)

def layer_norm(hidden):
    center = hidden - lax.optimization_barrier(jnp.mean(hidden, -1, keepdims=True))
    return center * lax.rsqrt(lax.optimization_barrier(jnp.mean(center * center, -1, keepdims=True)) + 1e-05)

def smooth_abs(delta):
    return jnp.sqrt(delta * delta + 0.0625)

def slope(delta):
    return delta / smooth_abs(delta)

def reference(latent, grid_embed, edge_src, area, target, w_query, w_keyval, w_head):
    members = latent.shape[0]
    rows = grid_embed.shape[0]
    width = grid_embed.shape[1]
    block = math.gcd(rows, 512)
    blocks = rows // block
    query = jnp.dot(grid_embed, w_query, preferred_element_type=jnp.float32)
    query_blocks = query.reshape(blocks, block, width)
    source_blocks = edge_src.reshape(blocks, block, KNB)
    embed_wide = grid_embed.astype(jnp.float32)

    def make_table(member_latent):
        rounded = jnp.dot(member_latent, w_keyval, preferred_element_type=jnp.float32).astype(jnp.bfloat16)
        return lax.optimization_barrier(rounded).astype(jnp.float32)

    def forward_hidden(table):
        mixed = lax.map(lambda pair: attend(pair[0], table, pair[1]), (query_blocks, source_blocks))
        return embed_wide + mixed.reshape(rows, width)

    def forward(member_latent):
        hidden = forward_hidden(make_table(member_latent))
        normed = layer_norm(hidden).astype(jnp.bfloat16)
        return jnp.dot(normed, w_head, preferred_element_type=jnp.float32)
    preds = lax.map(forward, latent)
    miss = preds - target[None]
    pair_value = jnp.zeros_like(preds)
    pair_slope = jnp.zeros_like(preds)
    for other in range(members):
        delta = preds - preds[other][None]
        pair_value = pair_value + smooth_abs(delta)
        pair_slope = pair_slope + slope(delta)
    pair_value = pair_value - 0.25
    weights = area[None, :, None]
    crps_terms = smooth_abs(miss) / members - pair_value / (2.0 * members * (members - 1))
    loss = lax.optimization_barrier(jnp.sum(weights * crps_terms, axis=(1, 2))) / (rows * target.shape[1])
    d_pred = weights * (slope(miss) / members - pair_slope / (members * (members - 1)))

    def backward(pair):
        member_latent, d_out = pair
        table = make_table(member_latent)
        hidden = forward_hidden(table)
        normed = layer_norm(hidden).astype(jnp.bfloat16)
        d_outb = d_out.astype(jnp.bfloat16)
        grad_h = jnp.dot(normed.T, d_outb, preferred_element_type=jnp.float32)
        d_normed = jnp.dot(d_outb, w_head.T, preferred_element_type=jnp.float32)
        ignored, norm_back = jax.vjp(layer_norm, hidden)
        d_hidden = norm_back(d_normed)[0]

        def block_back(carry, items):
            query_part, source_part, d_part = items
            ignored_out, attend_back = jax.vjp(lambda qq, tt: attend(qq, tt, source_part), query_part, table)
            d_q, d_t = attend_back(d_part)
            return (carry + d_t, d_q)
        d_table, d_query = lax.scan(block_back, jnp.zeros(table.shape, jnp.float32), (query_blocks, source_blocks, d_hidden.reshape(blocks, block, width)))
        d_queryb = d_query.reshape(rows, width).astype(jnp.bfloat16)
        d_tableb = d_table.astype(jnp.bfloat16)
        grad_q = jnp.dot(grid_embed.T, d_queryb, preferred_element_type=jnp.float32)
        grad_kv = jnp.dot(member_latent.T, d_tableb, preferred_element_type=jnp.float32)
        d_lat = jnp.dot(d_tableb, w_keyval.T, preferred_element_type=jnp.float32)
        return (grad_q, grad_kv, grad_h, d_lat)
    grad_q, grad_kv, grad_h, d_latent = lax.map(backward, (latent, d_pred))
    scale = (members * rows) ** (-0.5)
    return (loss, d_latent, lax.optimization_barrier(jnp.sum(grad_q, 0)) * scale, lax.optimization_barrier(jnp.sum(grad_kv, 0)) * scale, lax.optimization_barrier(jnp.sum(grad_h, 0)) * scale)
```

```python
import jax
import jax.numpy as jnp
from jax import lax
from jax.experimental import pallas as pl
from jax.experimental.pallas import tpu as pltpu
from jax.sharding import PartitionSpec as P

F32 = jnp.float32
BF16 = jnp.bfloat16
TILE = 128
SIZE = 64
MEMBERS = 8
SHARDS = 32
NODES = 32
WIDE = 96
ROWS = 256
WIDTH = 1024
VARS = 100
PAIR = 1.0 / (MEMBERS * (MEMBERS - 1))
SCALE = (MEMBERS * ROWS * SHARDS) ** (-0.5)
VMEM = pl.BlockSpec(memory_space=pltpu.VMEM)
SMEM = pl.BlockSpec(memory_space=pltpu.SMEM)


def dot(left, right, over=((1,), (0,))):
    return lax.dot_general(left, right, (over, ((), ())), preferred_element_type=F32)


def call(body, outs, specs, scratch=(), flops=0, size=0):
    return pl.pallas_call(
        body,
        out_shape=outs,
        in_specs=specs,
        out_specs=[VMEM] * len(outs),
        scratch_shapes=list(scratch),
        compiler_params=pltpu.CompilerParams(vmem_limit_bytes=48 * 1024 * 1024),
        cost_estimate=pl.CostEstimate(flops=flops, bytes_accessed=size, transcendentals=0),
    )


def lanes(shape):
    return lax.broadcasted_iota(jnp.int32, shape, len(shape) - 1)


def averager():
    row = lax.broadcasted_iota(jnp.int32, (TILE, TILE), 0) // SIZE
    return jnp.where(row == lanes((TILE, TILE)) // SIZE, 1.0 / SIZE, 0.0).astype(BF16)


def head_mean(values, average):
    high = values.astype(BF16)
    low = (values - high.astype(F32)).astype(BF16)
    return dot(high, average) + dot(low, average)


def counts_of(index):
    lane = lanes((ROWS, TILE))
    total = jnp.zeros((ROWS, TILE), F32)
    for k in range(3):
        total = total + jnp.where(index[:, k : k + 1] == lane, 1.0, 0.0)
    return total


def both_heads(tile):
    first = lanes(tile.shape) < SIZE
    zero = jnp.zeros_like(tile)
    return jnp.concatenate([jnp.where(first, tile, zero), jnp.where(first, zero, tile)], 0)


def pad_rows(tile):
    return jnp.concatenate([tile, jnp.zeros((TILE - tile.shape[0], tile.shape[1]), tile.dtype)], 0)


def per_head(first, second, shape):
    return jnp.where(lanes(shape) < SIZE, first, second)


def halves(values):
    return (
        jnp.sum(values[:, :TILE], -1, keepdims=True),
        jnp.sum(values[:, TILE:], -1, keepdims=True),
    )


def query_kernel(me, embed, w_query, normal, tile, inverse):
    average = averager()
    value = dot(embed[...], w_query[...])
    here = me[0]
    held = jnp.zeros((ROWS, TILE), F32)
    for t in range(WIDTH // TILE):
        part = value[:, t * TILE : (t + 1) * TILE]
        root = lax.rsqrt(head_mean(part * part, average) + 1e-06)
        normal[:, t * TILE : (t + 1) * TILE] = (part * root).astype(BF16)
        held = jnp.where(here == t, root, held)
    inverse[...] = held
    tile[...] = normal[:, pl.ds(pl.multiple_of(here * TILE, TILE), TILE)]


def forward_kernel(wide, w_keyval, normal, embed, index, w_head, payload, hidden):
    average = averager()
    count = counts_of(index[...])
    count = jnp.concatenate([count, count], 1)
    table = dot(wide[...], w_keyval[...]).astype(BF16)
    for t in range(WIDTH // TILE):
        at = slice(t * TILE, (t + 1) * TILE)
        key = table[:, at].astype(F32)
        key = (key * lax.rsqrt(head_mean(key * key, average) + 1e-06)).astype(BF16)
        key = both_heads(pad_rows(key))
        value = both_heads(pad_rows(table[:, WIDTH + t * TILE : WIDTH + (t + 1) * TILE]))
        score = dot(normal[:, at], key, ((1,), (1,)))
        expon = count * jnp.exp(score * SIZE**-0.5)
        first, second = halves(expon)
        mixed = dot(expon.astype(BF16), value)
        mixed = mixed * per_head(1.0 / first, 1.0 / second, mixed.shape)
        hidden[:, at] = embed[:, at].astype(F32) + mixed
    whole = hidden[...]
    mean = jnp.mean(whole, -1, keepdims=True)
    center = whole - mean
    inverse = lax.rsqrt(jnp.mean(center * center, -1, keepdims=True) + 1e-05)
    pred = dot((center * inverse).astype(BF16), w_head[...])
    lane = lanes(pred.shape)
    for at, stat in ((VARS, mean), (VARS + 2, inverse)):
        high = stat.astype(BF16).astype(F32)
        pred = jnp.where(lane == at, high, pred)
        pred = jnp.where(lane == at + 1, stat - high, pred)
    payload[...] = pred.astype(BF16)


def crps(preds, target, area, d_pred, lost):
    size = 32

    @pl.loop(0, ROWS // size)
    def _(step):
        rows = pl.ds(pl.multiple_of(step * size, size), size)
        value = [preds[k][rows, :].astype(F32) for k in range(MEMBERS)]
        slope = [jnp.zeros((size, TILE), F32) for _ in range(MEMBERS)]
        weight = jnp.where(lanes((size, TILE)) < VARS, area[rows, :], 0.0)
        aim = target[rows, :]
        pair = jnp.zeros((size, TILE), F32)
        for i in range(MEMBERS):
            for j in range(i + 1, MEMBERS):
                delta = value[i] - value[j]
                square = delta * delta + 0.0625
                root = lax.rsqrt(square)
                if i == 0:
                    pair = pair + square * root
                part = delta * root
                slope[i] = slope[i] + part
                slope[j] = slope[j] - part
        for i in range(MEMBERS):
            delta = value[i] - aim
            square = delta * delta + 0.0625
            root = lax.rsqrt(square)
            if i == 0:
                lost[rows, :] = weight * (square * root / MEMBERS - 0.5 * PAIR * pair)
            d_pred[i, rows, :] = (weight * (delta * root / MEMBERS - PAIR * slope[i])).astype(BF16)


def backward_kernel(
    me, latents, w_keyval, normal, inverse, embed, embed_tile, index, head_rows, head_sum,
    target, area, p0, p1, p2, p3, p4, p5, p6, p7,
    payload, t0, t1, t2, t3, t4, t5, t6, t7, d_pred, lost, d_table,
):
    preds = (p0, p1, p2, p3, p4, p5, p6, p7)
    tables = (t0, t1, t2, t3, t4, t5, t6, t7)
    here = me[0]
    crps(preds, target, area, d_pred, lost)
    average = averager()
    count = counts_of(index[...])
    count = jnp.concatenate([count, count], 1)
    query = normal[...]
    base = embed_tile[...].astype(F32)
    d_query = jnp.zeros((ROWS, TILE), F32)
    d_head = jnp.zeros((TILE, TILE), F32)
    shape = (ROWS, TILE)
    first_head = lanes((TILE, TILE)) < SIZE
    for k in range(MEMBERS):
        who = jnp.bitwise_xor(here, k)
        latent = latents[who]
        table = dot(latent, w_keyval[...]).astype(BF16)
        key_raw = pad_rows(table[:, :TILE]).astype(F32)
        key_root = lax.rsqrt(head_mean(key_raw * key_raw, average) + 1e-06)
        key_norm = key_raw * key_root
        key = both_heads(key_norm.astype(BF16))
        value = both_heads(pad_rows(table[:, TILE:]))
        score = dot(query, key, ((1,), (1,)))
        expon = count * jnp.exp(score * SIZE**-0.5)
        first, second = halves(expon)
        weight = jnp.concatenate([expon[:, :TILE] / first, expon[:, TILE:] / second], 1)
        weight_low = weight.astype(BF16)
        mixed = dot(weight_low, value)
        pred = preds[k][...].astype(F32)
        mean = pred[:, VARS : VARS + 1] + pred[:, VARS + 1 : VARS + 2]
        scale = pred[:, VARS + 2 : VARS + 3] + pred[:, VARS + 3 : VARS + 4]
        normed = (base + mixed - mean) * scale
        out = d_pred[k]
        out_wide = out.astype(F32)
        d_head = d_head + dot(normed.astype(BF16), out, ((0,), (0,)))
        d_normed = dot(out, head_rows[...], ((1,), (1,)))
        level = jnp.sum(out_wide * head_sum[...], -1, keepdims=True) / WIDTH
        along = jnp.sum(out_wide * pred, -1, keepdims=True) / WIDTH
        d_mixed = (scale * (d_normed - level - normed * along)).astype(BF16)
        d_weight = dot(d_mixed, value, ((1,), (1,)))
        first, second = halves(weight * d_weight)
        d_score = jnp.concatenate(
            [
                weight[:, :TILE] * (d_weight[:, :TILE] - first),
                weight[:, TILE:] * (d_weight[:, TILE:] - second),
            ],
            1,
        )
        d_score = (d_score * SIZE**-0.5).astype(BF16)
        d_value = dot(weight_low, d_mixed, ((0,), (0,)))
        d_value = jnp.where(first_head, d_value[:TILE], d_value[TILE:])
        d_query = d_query + dot(d_score, key)
        d_key = dot(d_score, query, ((0,), (0,)))
        d_key = jnp.where(first_head, d_key[:TILE], d_key[TILE:])
        d_key = key_root * (d_key - key_norm * head_mean(d_key * key_norm, average))
        both = jnp.concatenate([d_key[:WIDE], d_value[:WIDE]], 1).astype(BF16)
        tables[k][...] = both
        d_table[pl.ds(pl.multiple_of(who * WIDE, WIDE), WIDE), :] = both
    wide_query = query.astype(F32)
    d_query = inverse[...] * (d_query - wide_query * head_mean(d_query * wide_query, average))
    grad = dot(embed[...], d_query.astype(BF16), ((0,), (0,)))
    payload[:, :TILE] = (grad * SCALE).astype(BF16)
    flat = latents[...].reshape(MEMBERS * WIDE, WIDTH)
    grad = dot(flat, d_table[...], ((0,), (0,)))
    payload[:, TILE : 3 * TILE] = (grad * SCALE).astype(BF16)
    loss = jnp.sum(lost[...], axis=(0, 1), keepdims=True) / (ROWS * SHARDS * VARS)
    high = loss.astype(BF16).astype(F32)
    lane = lanes((WIDTH, TILE))
    side = jnp.where(lane == VARS, high, jnp.where(lane == VARS + 1, loss - high, 0.0))
    payload[:, 3 * TILE :] = side.astype(BF16)
    rows = pl.ds(pl.multiple_of(here * TILE, TILE), TILE)
    lane = lanes((TILE, TILE))
    payload[rows, 3 * TILE :] = jnp.where(
        lane < VARS, d_head * SCALE, side[:TILE]
    ).astype(BF16)


def sum_kernel(pieces, total, loss):
    value = jnp.sum(pieces[...].astype(F32), 0)
    total[...] = value.astype(BF16)
    loss[...] = value[0:1, 3 * TILE + VARS : 3 * TILE + VARS + 1] + value[
        0:1, 3 * TILE + VARS + 1 : 3 * TILE + VARS + 2
    ]


def place_kernel(me, g0, g1, g2, g3, g4, g5, g6, g7, query, keyval, head):
    here = me[0]
    total = jnp.zeros((NODES, TILE), F32)
    for k, part in enumerate((g0, g1, g2, g3, g4, g5, g6, g7)):
        at = pl.multiple_of(jnp.bitwise_xor(here, k) * TILE, TILE)
        query[:, pl.ds(at, TILE)] = part[:, :TILE].astype(F32)
        keyval[:, pl.ds(at, TILE)] = part[:, TILE : 2 * TILE].astype(F32)
        keyval[:, pl.ds(pl.multiple_of(WIDTH + at, TILE), TILE)] = part[
            :, 2 * TILE : 3 * TILE
        ].astype(F32)
        total = total + part[:, 3 * TILE :].astype(F32)
    head[...] = total[:, :VARS]


def latent_kernel(me, t0, t1, t2, t3, t4, t5, t6, t7, w_keyval, own, partner, other):
    here = me[0]
    total = jnp.zeros((WIDE, WIDTH), F32)
    for k, part in enumerate((t0, t1, t2, t3, t4, t5, t6, t7)):
        at = pl.multiple_of(jnp.bitwise_xor(here, k) * TILE, TILE)
        total = total + dot(part[:, :TILE], w_keyval[:, pl.ds(at, TILE)], ((1,), (1,)))
        at = pl.multiple_of(WIDTH + at, TILE)
        total = total + dot(part[:, TILE:], w_keyval[:, pl.ds(at, TILE)], ((1,), (1,)))
    own[...] = total[:NODES]
    partner[...] = total[NODES : 2 * NODES]
    other[...] = total[2 * NODES :].astype(BF16)


def swap(array, axis, bits):
    count = lax.axis_size(axis)
    return lax.ppermute(array, axis, [(i, i ^ bits) for i in range(count)])


def outward(sign):
    step = lambda i: 2 * sign if i % 2 == 0 else -2 * sign
    return [(i, (i + step(i)) % SHARDS) for i in range(SHARDS)]


def spread(array):
    slots = {0: array}
    for k in (6, 4, 2):
        slots[k] = swap(array, "member", k)
    for k in (0, 2, 4, 6):
        slots[k + 1] = swap(slots[k], "member", 1)
    return [slots[k] for k in range(MEMBERS)]


def shape(*dims, kind=BF16):
    return jax.ShapeDtypeStruct(dims, kind)


def on_device(latent, grid_embed, edge_src, area, target, w_query, w_keyval, w_head):
    member = lax.axis_index("member").astype(jnp.int32)
    shard = lax.axis_index("shard").astype(jnp.int32)
    me = member.reshape(1)
    own = latent[0]
    partner = swap(own, "shard", 1)
    other = lax.ppermute(partner, "shard", outward(1))
    wide = jnp.concatenate([own, partner, other], 0)
    offset = jnp.mod(edge_src // NODES - shard, SHARDS)
    toward = jnp.where(shard % 2 == 0, 1, SHARDS - 1)
    slot = jnp.where(offset == 0, 0, jnp.where(offset == toward, 1, 2))
    index = slot * NODES + edge_src % NODES
    head_wide = jnp.pad(w_head, ((0, 0), (0, TILE - VARS)))
    head_rows = lax.dynamic_slice_in_dim(head_wide, member * TILE, TILE, 0)
    head_sum = jnp.sum(head_wide.astype(F32), 0, keepdims=True)
    target_wide = jnp.pad(target, ((0, 0), (0, TILE - VARS)))
    area_wide = area[:, None]
    embed_tile = lax.dynamic_slice_in_dim(grid_embed, member * TILE, TILE, 1)
    keyval_tile = jnp.concatenate(
        [
            lax.dynamic_slice_in_dim(w_keyval, member * TILE, TILE, 1),
            lax.dynamic_slice_in_dim(w_keyval, WIDTH + member * TILE, TILE, 1),
        ],
        1,
    )
    normal, normal_tile, inverse = call(
        query_kernel,
        [shape(ROWS, WIDTH), shape(ROWS, TILE), shape(ROWS, TILE, kind=F32)],
        [SMEM, VMEM, VMEM],
        flops=2 * ROWS * WIDTH * WIDTH,
        size=4 << 20,
    )(me, grid_embed, w_query)
    (payload,) = call(
        forward_kernel,
        [shape(ROWS, TILE)],
        [VMEM] * 6,
        [pltpu.VMEM((ROWS, WIDTH), F32)],
        flops=4 << 30,
        size=8 << 20,
    )(wide, w_keyval, normal, grid_embed, index, head_wide)
    latents = lax.all_gather(wide, "member", axis=0, tiled=False)
    preds = spread(payload)
    results = call(
        backward_kernel,
        [shape(WIDTH, 4 * TILE)] + [shape(WIDE, 2 * TILE)] * MEMBERS,
        [SMEM] + [VMEM] * 19,
        [
            pltpu.VMEM((MEMBERS, ROWS, TILE), BF16),
            pltpu.VMEM((ROWS, TILE), F32),
            pltpu.VMEM((MEMBERS * WIDE, 2 * TILE), BF16),
        ],
        flops=8 << 30,
        size=16 << 20,
    )(
        me, latents, keyval_tile, normal_tile, inverse, grid_embed, embed_tile, index,
        head_rows, head_sum, target_wide, area_wide, *preds,
    )
    grads, d_tables = results[0], results[1:]
    d_tables = [d_tables[0]] + [swap(d_tables[k], "member", k) for k in range(1, MEMBERS)]
    pieces = lax.all_to_all(
        grads.reshape(SHARDS, NODES, 4 * TILE), "shard", 0, 0, tiled=False
    )
    total, loss = call(
        sum_kernel,
        [shape(NODES, 4 * TILE), shape(1, 1, kind=F32)],
        [VMEM],
        flops=1 << 20,
        size=1 << 20,
    )(pieces)
    parts = spread(total)
    grad_query, grad_keyval, grad_head = call(
        place_kernel,
        [
            shape(NODES, WIDTH, kind=F32),
            shape(NODES, 2 * WIDTH, kind=F32),
            shape(NODES, VARS, kind=F32),
        ],
        [SMEM] + [VMEM] * MEMBERS,
        size=1 << 20,
    )(me, *parts)
    mine, near, far = call(
        latent_kernel,
        [
            shape(NODES, WIDTH, kind=F32),
            shape(NODES, WIDTH, kind=F32),
            shape(NODES, WIDTH),
        ],
        [SMEM] + [VMEM] * 9,
        flops=2 * WIDE * WIDTH * 2 * WIDTH,
        size=5 << 20,
    )(me, *d_tables, w_keyval)
    near = near + lax.ppermute(far, "shard", outward(-1)).astype(F32)
    d_latent = mine + swap(near.astype(BF16), "shard", 1).astype(F32)
    return (loss.reshape(1), d_latent[None], grad_query, grad_keyval, grad_head)


def solution(mesh):
    placed = (
        P("member", "shard", None),
        P("shard", None),
        P("shard", None),
        P("shard"),
        P("shard", None),
        P(),
        P(),
        P(),
    )
    return jax.shard_map(
        on_device,
        mesh=mesh,
        in_specs=placed,
        out_specs=(
            P("member"),
            P("member", "shard", None),
            P("shard", None),
            P("shard", None),
            P("shard", None),
        ),
        check_vma=False,
    )
```

```python
import jax
import jax.numpy as jnp
from jax import lax
from jax.experimental import pallas as pl
from jax.experimental.pallas import tpu as pltpu
from jax.sharding import PartitionSpec as P

F32 = jnp.float32
BF16 = jnp.bfloat16
TILE = 128
SIZE = 64
TILES = 8
MEMBERS = 8
SHARDS = 32
NODES = 32
WIDE = 96
BOTH = 2 * WIDE
ROWS = 256
WIDTH = 1024
VARS = 100
CARRY = 112
PAIR = 1.0 / (MEMBERS * (MEMBERS - 1))
SCALE = (MEMBERS * ROWS * SHARDS) ** (-0.5)
VMEM = pl.BlockSpec(memory_space=pltpu.VMEM)
SMEM = pl.BlockSpec(memory_space=pltpu.SMEM)


def dot(left, right):
    return lax.dot_general(left, right, (((1,), (0,)), ((), ())), preferred_element_type=F32)


def dot_nt(left, right):
    return lax.dot_general(left, right, (((1,), (1,)), ((), ())), preferred_element_type=F32)


def dot_tn(left, right):
    return lax.dot_general(left, right, (((0,), (0,)), ((), ())), preferred_element_type=F32)


def call(body, outs, specs, scratch=(), flops=0, size=0):
    return pl.pallas_call(
        body,
        out_shape=outs,
        in_specs=specs,
        out_specs=[VMEM] * len(outs),
        scratch_shapes=list(scratch),
        compiler_params=pltpu.CompilerParams(vmem_limit_bytes=40 * 1024 * 1024),
        cost_estimate=pl.CostEstimate(flops=flops, bytes_accessed=size, transcendentals=0),
    )


def iota(shape, dim):
    return lax.broadcasted_iota(jnp.int32, shape, dim)


def lane_mean(values):
    average = jnp.where(
        iota((TILE, TILE), 0) // SIZE == iota((TILE, TILE), 1) // SIZE, 1.0 / SIZE, 0.0
    ).astype(BF16)
    high = values.astype(BF16)
    low = (values - high.astype(F32)).astype(BF16)
    return dot(high, average) + dot(low, average)


def stack_heads(tile):
    first = iota(tile.shape, 1) < SIZE
    zero = jnp.zeros_like(tile)
    return jnp.concatenate([jnp.where(first, tile, zero), jnp.where(first, zero, tile)], 0)


def unstack_heads(both):
    first = iota((WIDE, TILE), 1) < SIZE
    return jnp.where(first, both[:WIDE], both[WIDE:])


def per_half(values, size, first, second):
    return jnp.concatenate([values[:size] * first, values[size:] * second], 0)


def half_sums(values):
    return (
        jnp.sum(values[:WIDE], 0, keepdims=True),
        jnp.sum(values[WIDE:], 0, keepdims=True),
    )


def key_parts(raw):
    root = lax.rsqrt(lane_mean(raw * raw) + 1e-06)
    return raw * root, root


def attention(query, key, value, count):
    score = dot(key, query)
    expon = jnp.exp(score * SIZE**-0.5)
    expon = jnp.concatenate([expon[:WIDE] * count, expon[WIDE:] * count], 0)
    first, second = half_sums(expon)
    weight = per_half(expon, WIDE, 1.0 / first, 1.0 / second).astype(BF16)
    return weight, dot_tn(value, weight)


def attention_back(weight, value, query, d_mixed):
    d_weight = dot(value, d_mixed)
    wide = weight.astype(F32)
    first, second = half_sums(wide * d_weight)
    d_score = jnp.concatenate([d_weight[:WIDE] - first, d_weight[WIDE:] - second], 0)
    d_score = (wide * d_score * SIZE**-0.5).astype(BF16)
    return d_score, unstack_heads(dot_nt(weight, d_mixed)), unstack_heads(dot_nt(d_score, query))


def key_back(d_key, normal, root):
    return root * (d_key - normal * lane_mean(d_key * normal))


def norm_back(d_normed, normed, d_pred, pred, head_sum, scale):
    wide = d_pred.astype(F32)
    level = jnp.sum(wide * head_sum, 0, keepdims=True) / WIDTH
    along = jnp.sum(wide * pred, 0, keepdims=True) / WIDTH
    return (scale * (d_normed - level - normed * along)).astype(BF16)


def stats_of(payload):
    pred = payload.astype(F32)
    mean = pred[VARS : VARS + 1] + pred[VARS + 1 : VARS + 2]
    scale = pred[VARS + 2 : VARS + 3] + pred[VARS + 3 : VARS + 4]
    return pred, mean, scale


def prepare_kernel(
    me, embed, w_query, w_keyval, w_head, edges, target,
    normal, normal_tile, inverse, embed_turned, embed_tile, keyval_tile,
    head_turned, head, head_tile, head_sum, count, aim,
):
    here = me[0]
    shard = me[1]
    at = pl.multiple_of(here * TILE, TILE)
    embed_turned[...] = embed[...].T
    embed_tile[...] = embed_turned[pl.ds(at, TILE), :]
    value = dot(embed[...], w_query[...]).T
    held = jnp.zeros((TILE, ROWS), F32)
    for t in range(TILES):
        roots = []
        for h in (2 * t, 2 * t + 1):
            part = value[h * SIZE : (h + 1) * SIZE]
            root = lax.rsqrt(jnp.mean(part * part, 0, keepdims=True) + 1e-06)
            normal[h * SIZE : (h + 1) * SIZE, :] = (part * root).astype(BF16)
            roots.append(jnp.broadcast_to(root, (SIZE, ROWS)))
        held = jnp.where(here == t, jnp.concatenate(roots, 0), held)
    inverse[...] = held
    normal_tile[...] = normal[pl.ds(at, TILE), :]
    keyval_tile[:, :TILE] = w_keyval[:, pl.ds(at, TILE)]
    keyval_tile[:, TILE:] = w_keyval[:, pl.ds(pl.multiple_of(WIDTH + at, TILE), TILE)]
    rows = jnp.concatenate([w_head[...], jnp.zeros((TILE - VARS, WIDTH), BF16)], 0)
    head_turned[...] = rows[:CARRY]
    head[...] = rows.T
    head_tile[...] = head[pl.ds(at, TILE), :]
    head_sum[...] = jnp.sum(rows.astype(F32), 1, keepdims=True)
    source = edges[...]
    offset = jnp.bitwise_and(jnp.right_shift(source, 5) - shard + SHARDS, SHARDS - 1)
    toward = jnp.where(jnp.bitwise_and(shard, 1) == 0, 1, SHARDS - 1)
    slot = jnp.where(offset == 0, 0, jnp.where(offset == toward, 1, 2))
    index = slot * NODES + jnp.bitwise_and(source, NODES - 1)
    node = iota((WIDE, ROWS), 0)
    total = jnp.zeros((WIDE, ROWS), F32)
    for k in range(3):
        total = total + jnp.where(index[k : k + 1] == node, 1.0, 0.0)
    count[...] = total
    aim[...] = jnp.concatenate([target[...], jnp.zeros((CARRY - VARS, ROWS), F32)], 0)


def forward_kernel(
    own, partner, other, w_keyval, normal, embed, count, head_turned,
    payload, weights, normed, keys, key_roots, values, hidden,
):
    counts = count[...]
    wide = jnp.concatenate([own[...], partner[...], other[...]], 0)
    table = dot(wide, w_keyval[...]).astype(BF16)
    for t in range(TILES):
        at = slice(t * TILE, (t + 1) * TILE)
        key, root = key_parts(table[:, at].astype(F32))
        value = table[:, WIDTH + t * TILE : WIDTH + (t + 1) * TILE]
        keys[:, at] = key.astype(BF16)
        key_roots[:, at] = root
        values[:, at] = value
        weight, mixed = attention(
            normal[at, :], stack_heads(key.astype(BF16)), stack_heads(value), counts
        )
        weights[t] = weight
        hidden[at, :] = embed[at, :].astype(F32) + mixed
    whole = hidden[...]
    mean = jnp.mean(whole, 0, keepdims=True)
    center = whole - mean
    scale = lax.rsqrt(jnp.mean(center * center, 0, keepdims=True) + 1e-05)
    result = (center * scale).astype(BF16)
    normed[...] = result
    pred = dot(head_turned[...], result)
    row = iota(pred.shape, 0)
    for at, stat in ((VARS, mean), (VARS + 2, scale)):
        high = stat.astype(BF16).astype(F32)
        pred = jnp.where(row == at, high, pred)
        pred = jnp.where(row == at + 1, stat - high, pred)
    payload[...] = pred.astype(BF16)


def tables_kernel(*refs):
    latents = refs[: 3 * MEMBERS]
    keyval_tile, normal_tile, embed_tile, count = refs[3 * MEMBERS : 3 * MEMBERS + 4]
    turned, weights, keys, key_roots, values, hidden, flat = refs[3 * MEMBERS + 4 :]
    for i, latent in enumerate(latents):
        flat[i * NODES : (i + 1) * NODES, :] = latent[...]
    turned[...] = flat[...].T
    table = dot(flat[...], keyval_tile[...]).astype(BF16)
    counts = count[...]
    query = normal_tile[...]
    base = embed_tile[...].astype(F32)
    for k in range(MEMBERS):
        part = table[k * WIDE : (k + 1) * WIDE]
        key, root = key_parts(part[:, :TILE].astype(F32))
        keys[k] = key.astype(BF16)
        key_roots[k] = root
        values[k] = part[:, TILE:]
        weight, mixed = attention(
            query, stack_heads(key.astype(BF16)), stack_heads(part[:, TILE:]), counts
        )
        weights[k] = weight
        hidden[k] = base + mixed


def crps(preds, target, area, d_pred, lost):
    size = 16
    d_pred[:, CARRY:, :] = jnp.zeros((MEMBERS, TILE - CARRY, ROWS), BF16)

    @pl.loop(0, CARRY // size)
    def _(step):
        start = pl.multiple_of(step * size, size)
        rows = pl.ds(start, size)
        for side in range(0, ROWS, TILE):
            cols = slice(side, side + TILE)
            value = [preds[k][rows, cols].astype(F32) for k in range(MEMBERS)]
            slope = [jnp.zeros((size, TILE), F32) for _ in range(MEMBERS)]
            weight = jnp.where(iota((size, TILE), 0) + start < VARS, area[:, cols], 0.0)
            aim = target[rows, cols]
            pair = jnp.zeros((size, TILE), F32)
            for i in range(MEMBERS):
                for j in range(i + 1, MEMBERS):
                    delta = value[i] - value[j]
                    square = delta * delta + 0.0625
                    root = lax.rsqrt(square)
                    if i == 0:
                        pair = pair + square * root
                    part = delta * root
                    slope[i] = slope[i] + part
                    slope[j] = slope[j] - part
            for i in range(MEMBERS):
                delta = value[i] - aim
                square = delta * delta + 0.0625
                root = lax.rsqrt(square)
                if i == 0:
                    lost[rows, cols] = weight * (square * root / MEMBERS - 0.5 * PAIR * pair)
                d_pred[i, rows, cols] = (
                    weight * (delta * root / MEMBERS - PAIR * slope[i])
                ).astype(BF16)


def backward_kernel(
    me, turned, weights, keys, key_roots, values, hidden, normal_tile, inverse, embed_turned,
    head_tile, head_sum, target, area, p0, p1, p2, p3, p4, p5, p6, p7,
    payload, d_own, d_pred, lost, d_table,
):
    preds = (p0, p1, p2, p3, p4, p5, p6, p7)
    here = me[0]
    crps(preds, target, area, d_pred, lost)
    d_own[...] = d_pred[0]
    query = normal_tile[...]
    sums = head_sum[...]
    d_query = jnp.zeros((TILE, ROWS), F32)
    d_head = jnp.zeros((TILE, TILE), F32)
    for k in range(MEMBERS):
        pred, mean, scale = stats_of(preds[k][...])
        normed = (hidden[k] - mean) * scale
        out = d_pred[k]
        d_head = d_head + dot_nt(normed.astype(BF16), out)
        d_mixed = norm_back(
            dot(head_tile[...], out), normed, out[:CARRY], pred, sums[:CARRY], scale
        )
        key = keys[k]
        value = stack_heads(values[k])
        d_score, d_value, d_key = attention_back(weights[k], value, query, d_mixed)
        d_query = d_query + dot_tn(stack_heads(key), d_score)
        d_key = key_back(d_key, key.astype(F32), key_roots[k])
        rows = slice(k * WIDE, (k + 1) * WIDE)
        d_table[rows, :TILE] = d_key.astype(BF16)
        d_table[rows, TILE:] = d_value.astype(BF16)
    wide_query = query.astype(F32)
    along = d_query * wide_query
    along = jnp.concatenate(
        [
            jnp.broadcast_to(jnp.mean(along[:SIZE], 0, keepdims=True), (SIZE, ROWS)),
            jnp.broadcast_to(jnp.mean(along[SIZE:], 0, keepdims=True), (SIZE, ROWS)),
        ],
        0,
    )
    d_query = inverse[...] * (d_query - wide_query * along)
    grad = dot_nt(embed_turned[...], d_query.astype(BF16))
    payload[:, :TILE] = (grad * SCALE).astype(BF16)
    grad = dot(turned[...], d_table[...])
    payload[:, TILE : 3 * TILE] = (grad * SCALE).astype(BF16)
    loss = jnp.sum(lost[...], axis=(0, 1), keepdims=True) / (ROWS * SHARDS * VARS)
    high = loss.astype(BF16).astype(F32)
    lane = iota((WIDTH, TILE), 1)
    side = jnp.where(lane == VARS, high, jnp.where(lane == VARS + 1, loss - high, 0.0))
    payload[:, 3 * TILE :] = side.astype(BF16)
    rows = pl.ds(pl.multiple_of(here * TILE, TILE), TILE)
    payload[rows, 3 * TILE :] = jnp.where(
        iota((TILE, TILE), 1) < VARS, d_head * SCALE, side[:TILE]
    ).astype(BF16)


def latent_kernel(
    d_own, payload, weights, normed, keys, key_roots, values, normal, head, head_sum, w_keyval,
    own, partner, other, d_table,
):
    out = d_own[...]
    pred, mean, scale = stats_of(payload[...])
    d_normed = dot(head[...], out)
    d_mixed = norm_back(
        d_normed, normed[...].astype(F32), out[:CARRY], pred, head_sum[:CARRY], scale
    )
    for t in range(TILES):
        at = slice(t * TILE, (t + 1) * TILE)
        key = keys[:, at]
        d_score, d_value, d_key = attention_back(
            weights[t], stack_heads(values[:, at]), normal[at, :], d_mixed[at]
        )
        d_key = key_back(d_key, key.astype(F32), key_roots[:, at])
        d_table[:, at] = d_key.astype(BF16)
        d_table[:, WIDTH + t * TILE : WIDTH + (t + 1) * TILE] = d_value.astype(BF16)
    total = dot_nt(d_table[...], w_keyval[...])
    own[...] = total[:NODES]
    partner[...] = total[NODES : 2 * NODES]
    other[...] = total[2 * NODES :].astype(BF16)


def sum_kernel(pieces, total, loss):
    value = jnp.sum(pieces[...].astype(F32), 0)
    total[...] = value.astype(BF16)
    at = 3 * TILE + VARS
    loss[...] = value[0:1, at : at + 1] + value[0:1, at + 1 : at + 2]


def place_kernel(me, g0, g1, g2, g3, g4, g5, g6, g7, query, keyval, head):
    here = me[0]
    total = jnp.zeros((NODES, TILE), F32)
    for k, part in enumerate((g0, g1, g2, g3, g4, g5, g6, g7)):
        at = pl.multiple_of(jnp.bitwise_xor(here, k) * TILE, TILE)
        query[:, pl.ds(at, TILE)] = part[:, :TILE].astype(F32)
        keyval[:, pl.ds(at, TILE)] = part[:, TILE : 2 * TILE].astype(F32)
        keyval[:, pl.ds(pl.multiple_of(WIDTH + at, TILE), TILE)] = part[
            :, 2 * TILE : 3 * TILE
        ].astype(F32)
        total = total + part[:, 3 * TILE :].astype(F32)
    head[...] = total[:, :VARS]


def swap(array, axis, bits):
    count = lax.axis_size(axis)
    return lax.ppermute(array, axis, [(i, i ^ bits) for i in range(count)])


def outward(sign):
    step = lambda i: 2 * sign if i % 2 == 0 else -2 * sign
    return [(i, (i + step(i)) % SHARDS) for i in range(SHARDS)]


def spread(array):
    slots = {0: array}
    for k in (6, 4, 2):
        slots[k] = swap(array, "member", k)
    for k in (0, 2, 4, 6):
        slots[k + 1] = swap(slots[k], "member", 1)
    return [slots[k] for k in range(MEMBERS)]


def shape(*dims, kind=BF16):
    return jax.ShapeDtypeStruct(dims, kind)


def on_device(latent, grid_embed, edge_src, area, target, w_query, w_keyval, w_head):
    member = lax.axis_index("member").astype(jnp.int32)
    shard = lax.axis_index("shard").astype(jnp.int32)
    me = jnp.stack([member, shard])
    own = latent[0]
    partner = swap(own, "shard", 1)
    other = lax.ppermute(partner, "shard", outward(1))
    (
        normal, normal_tile, inverse, embed_turned, embed_tile, keyval_tile,
        head_turned, head, head_tile, head_sum, count, aim,
    ) = call(
        prepare_kernel,
        [
            shape(WIDTH, ROWS),
            shape(TILE, ROWS),
            shape(TILE, ROWS, kind=F32),
            shape(WIDTH, ROWS),
            shape(TILE, ROWS),
            shape(WIDTH, 2 * TILE),
            shape(CARRY, WIDTH),
            shape(WIDTH, TILE),
            shape(TILE, TILE),
            shape(TILE, 1, kind=F32),
            shape(WIDE, ROWS, kind=F32),
            shape(CARRY, ROWS, kind=F32),
        ],
        [SMEM] + [VMEM] * 6,
        flops=2 * ROWS * WIDTH * WIDTH,
        size=8 << 20,
    )(me, grid_embed, w_query, w_keyval, w_head.T, edge_src.T, target.T)
    payload, weights, normed, keys, key_roots, values = call(
        forward_kernel,
        [
            shape(CARRY, ROWS),
            shape(TILES, BOTH, ROWS),
            shape(WIDTH, ROWS),
            shape(WIDE, WIDTH),
            shape(WIDE, WIDTH, kind=F32),
            shape(WIDE, WIDTH),
        ],
        [VMEM] * 8,
        [pltpu.VMEM((WIDTH, ROWS), F32)],
        flops=1 << 30,
        size=8 << 20,
    )(own, partner, other, w_keyval, normal, embed_turned, count, head_turned)
    preds = spread(payload)
    blocks = [spread(part) for part in (own, partner, other)]
    latents = [blocks[i][k] for k in range(MEMBERS) for i in range(3)]
    member_parts = call(
        tables_kernel,
        [
            shape(WIDTH, MEMBERS * WIDE),
            shape(MEMBERS, BOTH, ROWS),
            shape(MEMBERS, WIDE, TILE),
            shape(MEMBERS, WIDE, TILE, kind=F32),
            shape(MEMBERS, WIDE, TILE),
            shape(MEMBERS, TILE, ROWS, kind=F32),
        ],
        [VMEM] * (3 * MEMBERS + 4),
        [pltpu.VMEM((MEMBERS * WIDE, WIDTH), BF16)],
        flops=2 << 30,
        size=8 << 20,
    )(*latents, keyval_tile, normal_tile, embed_tile, count)
    grads, d_own = call(
        backward_kernel,
        [shape(WIDTH, 4 * TILE), shape(TILE, ROWS)],
        [SMEM] + [VMEM] * 21,
        [
            pltpu.VMEM((MEMBERS, TILE, ROWS), BF16),
            pltpu.VMEM((CARRY, ROWS), F32),
            pltpu.VMEM((MEMBERS * WIDE, 2 * TILE), BF16),
        ],
        flops=2 << 30,
        size=8 << 20,
    )(
        me, *member_parts, normal_tile, inverse, embed_turned, head_tile, head_sum, aim,
        area.reshape(1, ROWS), *preds,
    )
    pieces = lax.all_to_all(
        grads.reshape(SHARDS, NODES, 4 * TILE), "shard", 0, 0, tiled=False
    )
    total, loss = call(
        sum_kernel,
        [shape(NODES, 4 * TILE), shape(1, 1, kind=F32)],
        [VMEM],
        flops=1 << 20,
        size=1 << 20,
    )(pieces)
    parts = spread(total)
    grad_query, grad_keyval, grad_head = call(
        place_kernel,
        [
            shape(NODES, WIDTH, kind=F32),
            shape(NODES, 2 * WIDTH, kind=F32),
            shape(NODES, VARS, kind=F32),
        ],
        [SMEM] + [VMEM] * MEMBERS,
        size=1 << 20,
    )(me, *parts)
    mine, near, far = call(
        latent_kernel,
        [
            shape(NODES, WIDTH, kind=F32),
            shape(NODES, WIDTH, kind=F32),
            shape(NODES, WIDTH),
        ],
        [VMEM] * 11,
        [pltpu.VMEM((WIDE, 2 * WIDTH), BF16)],
        flops=1 << 30,
        size=8 << 20,
    )(
        d_own, payload, weights, normed, keys, key_roots, values, normal, head, head_sum,
        w_keyval,
    )
    near = near + lax.ppermute(far, "shard", outward(-1)).astype(F32)
    d_latent = mine + swap(near.astype(BF16), "shard", 1).astype(F32)
    return (loss.reshape(1), d_latent[None], grad_query, grad_keyval, grad_head)


def solution(mesh):
    placed = (
        P("member", "shard", None),
        P("shard", None),
        P("shard", None),
        P("shard"),
        P("shard", None),
        P(),
        P(),
        P(),
    )
    return jax.shard_map(
        on_device,
        mesh=mesh,
        in_specs=placed,
        out_specs=(
            P("member"),
            P("member", "shard", None),
            P("shard", None),
            P("shard", None),
            P("shard", None),
        ),
        check_vma=False,
    )
```

```python
import jax
import jax.numpy as jnp
from jax import lax
from jax.experimental import pallas as pl
from jax.experimental.pallas import tpu as pltpu
from jax.sharding import PartitionSpec as P

F32 = jnp.float32
BF16 = jnp.bfloat16
TILE = 128
SIZE = 64
TILES = 8
MEMBERS = 8
HALF = 4
SHARDS = 32
NODES = 32
WIDE = 96
BOTH = 2 * WIDE
ROWS = 256
WIDTH = 1024
VARS = 100
KNB = 3
CARRY = 112
EDGE = 96
FOLDS = 4
PAIR = 1.0 / (MEMBERS * (MEMBERS - 1))
SCALE = (MEMBERS * ROWS * SHARDS) ** (-0.5)
VMEM = pl.BlockSpec(memory_space=pltpu.VMEM)
SMEM = pl.BlockSpec(memory_space=pltpu.SMEM)


def dot(left, right):
    return lax.dot_general(left, right, (((1,), (0,)), ((), ())), preferred_element_type=F32)


def dot_nt(left, right):
    return lax.dot_general(left, right, (((1,), (1,)), ((), ())), preferred_element_type=F32)


def dot_tn(left, right):
    return lax.dot_general(left, right, (((0,), (0,)), ((), ())), preferred_element_type=F32)


def call(body, outs, specs, scratch=(), flops=0, size=0, limit=12):
    return pl.pallas_call(
        body,
        out_shape=outs,
        in_specs=specs,
        out_specs=[VMEM] * len(outs),
        scratch_shapes=list(scratch),
        compiler_params=pltpu.CompilerParams(vmem_limit_bytes=limit << 20),
        cost_estimate=pl.CostEstimate(flops=flops, bytes_accessed=size, transcendentals=0),
    )


def iota(shape, dim):
    return lax.broadcasted_iota(jnp.int32, shape, dim)


def lane_mean(values):
    average = jnp.where(
        iota((TILE, TILE), 0) // SIZE == iota((TILE, TILE), 1) // SIZE, 1.0 / SIZE, 0.0
    ).astype(BF16)
    high = values.astype(BF16)
    low = (values - high.astype(F32)).astype(BF16)
    return dot(high, average) + dot(low, average)


def stack_heads(tile):
    first = iota(tile.shape, 1) < SIZE
    zero = jnp.zeros_like(tile)
    return jnp.concatenate([jnp.where(first, tile, zero), jnp.where(first, zero, tile)], 0)


def unstack_heads(both):
    first = iota((WIDE, TILE), 1) < SIZE
    return jnp.where(first, both[:WIDE], both[WIDE:])


def half_sums(values):
    return (
        jnp.sum(values[:WIDE], 0, keepdims=True),
        jnp.sum(values[WIDE:], 0, keepdims=True),
    )


def key_parts(raw):
    root = lax.rsqrt(lane_mean(raw * raw) + 1e-06)
    return raw * root, root


def attention_back(weight, value, query, d_mixed):
    d_weight = dot(value, d_mixed)
    wide = weight.astype(F32)
    first, second = half_sums(wide * d_weight)
    d_score = jnp.concatenate([d_weight[:WIDE] - first, d_weight[WIDE:] - second], 0)
    d_score = (wide * d_score * SIZE**-0.5).astype(BF16)
    return d_score, unstack_heads(dot_nt(weight, d_mixed)), unstack_heads(dot_nt(d_score, query))


def key_back(d_key, normal, root):
    return root * (d_key - normal * lane_mean(d_key * normal))


def counts_of(edges, shard):
    source = edges[...]
    offset = jnp.bitwise_and(jnp.right_shift(source, 5) - shard + SHARDS, SHARDS - 1)
    toward = jnp.where(jnp.bitwise_and(shard, 1) == 0, 1, SHARDS - 1)
    slot = jnp.where(offset == 0, 0, jnp.where(offset == toward, 1, 2))
    index = slot * NODES + jnp.bitwise_and(source, NODES - 1)
    node = iota((WIDE, ROWS), 0)
    total = jnp.zeros((WIDE, ROWS), F32)
    for k in range(KNB):
        total = total + jnp.where(index[k : k + 1] == node, 1.0, 0.0)
    return total


def prepare_kernel(
    me, embed, w_query, normal, normal_tile, inverse, embed_turned, embed_tile
):
    here = me[0]
    at = pl.multiple_of(here * TILE, TILE)
    embed_turned[...] = embed[...].T
    embed_tile[...] = embed_turned[pl.ds(at, TILE), :]
    value = dot(embed[...], w_query[...]).T
    held = jnp.zeros((TILE, ROWS), F32)
    for t in range(TILES):
        roots = []
        for h in (2 * t, 2 * t + 1):
            part = value[h * SIZE : (h + 1) * SIZE]
            root = lax.rsqrt(jnp.mean(part * part, 0, keepdims=True) + 1e-06)
            normal[h * SIZE : (h + 1) * SIZE, :] = (part * root).astype(BF16)
            roots.append(jnp.broadcast_to(root, (SIZE, ROWS)))
        held = jnp.where(here == t, jnp.concatenate(roots, 0), held)
    inverse[...] = held
    normal_tile[...] = normal[pl.ds(at, TILE), :]


def weigh(scores, count):
    groups = scores.shape[0] // WIDE
    expon = jnp.exp(scores * SIZE**-0.5).reshape(groups, WIDE, ROWS) * count[None]
    weight = expon * (1.0 / jnp.sum(expon, 1, keepdims=True))
    return weight.astype(BF16).reshape(groups * WIDE, ROWS)


def forward_kernel(
    me, own, partner, other, w_keyval, normal, embed, edges, w_head,
    bundle, weights, normed, table, hidden,
):
    bundle[:NODES, :] = other[...]
    counts = counts_of(edges, me[1])
    wide = jnp.concatenate([own[...], partner[...], other[...]], 0)
    low = dot(wide, w_keyval[...]).astype(BF16)
    table[...] = low
    tiles = [slice(t * TILE, (t + 1) * TILE) for t in range(TILES)]
    raw = jnp.concatenate([low[:, at] for at in tiles], 0).astype(F32)
    keys = key_parts(raw)[0].astype(BF16)
    scores = [
        dot(stack_heads(keys[t * WIDE : (t + 1) * WIDE]), normal[at, :])
        for t, at in enumerate(tiles)
    ]
    shares = [weigh(score, counts) for score in scores]
    for t, at in enumerate(tiles):
        weights[t] = shares[t]
        value = stack_heads(low[:, WIDTH + t * TILE : WIDTH + (t + 1) * TILE])
        hidden[at, :] = embed[at, :].astype(F32) + dot_tn(value, shares[t])
    whole = hidden[...]
    mean = jnp.mean(whole, 0, keepdims=True)
    center = whole - mean
    scale = lax.rsqrt(jnp.mean(center * center, 0, keepdims=True) + 1e-05)
    result = (center * scale).astype(BF16)
    normed[...] = result
    pred = dot(w_head[...], result)
    pred = jnp.concatenate([pred, jnp.zeros((TILE - VARS, ROWS), F32)], 0)
    row = iota(pred.shape, 0)
    for at, stat in ((VARS, mean), (VARS + 2, scale)):
        high = stat.astype(BF16).astype(F32)
        pred = jnp.where(row == at, high, pred)
        pred = jnp.where(row == at + 1, stat - high, pred)
    pred = pred.astype(BF16)
    for q in range(FOLDS):
        bundle[NODES:, q * ROWS : (q + 1) * ROWS] = pred[q * NODES : (q + 1) * NODES]


def stack_kernel(*refs):
    parts, out = refs[:-1], refs[-1]
    at = 0
    for b in range(len(parts) // HALF):
        rows = parts[b * HALF].shape[0]
        for i in range(HALF):
            out[i, at : at + rows, :] = parts[b * HALF + i][...]
        at += rows


def tables_kernel(
    me, stack, w_keyval, normal_tile, embed_tile, edges,
    turned, weights, keys, key_roots, values, hidden,
):
    at = pl.multiple_of(me[0] * TILE, TILE)
    flat = jnp.concatenate([stack[i, :WIDE, :] for i in range(HALF)], 0)
    turned[...] = flat.T
    key, root = key_parts(dot(flat, w_keyval[:, pl.ds(at, TILE)]).astype(BF16).astype(F32))
    at = pl.multiple_of(WIDTH + at, TILE)
    value = dot(flat, w_keyval[:, pl.ds(at, TILE)]).astype(BF16)
    key_roots[...] = root
    key = key.astype(BF16)
    members = [slice(i * WIDE, (i + 1) * WIDE) for i in range(HALF)]
    key = jnp.concatenate([stack_heads(key[rows]) for rows in members], 0)
    value = jnp.concatenate([stack_heads(value[rows]) for rows in members], 0)
    keys[...] = key
    values[...] = value
    weight = weigh(dot(key, normal_tile[...]), counts_of(edges, me[1]))
    weights[...] = weight
    base = embed_tile[...].astype(F32)
    for i in range(HALF):
        rows = slice(i * BOTH, (i + 1) * BOTH)
        hidden[i] = base + dot_tn(value[rows], weight[rows])


def head_kernel(me, w_head, head, head_tile, head_sum):
    at = pl.multiple_of(me[0] * TILE, TILE)
    rows = jnp.concatenate([w_head[...], jnp.zeros((TILE - VARS, WIDTH), BF16)], 0)
    head[...] = rows.T
    head_tile[...] = head[pl.ds(at, TILE), :]
    head_sum[...] = jnp.sum(rows.astype(F32), 1, keepdims=True)


def payload_rows(stack, i, start, size):
    fold, row = start // NODES, WIDE + start % NODES
    return stack[i, row : row + size, fold * ROWS : (fold + 1) * ROWS]


def stats_of(stack, i):
    rows = payload_rows(stack, i, EDGE, 16).astype(F32)
    at = VARS - EDGE
    mean = rows[at : at + 1] + rows[at + 1 : at + 2]
    return mean, rows[at + 2 : at + 3] + rows[at + 3 : at + 4]


def crps_kernel(mine, theirs, target, area, d_pred, d_own, loss):
    size = 16
    stacks = (mine, theirs)
    lost = jnp.zeros((size, ROWS), F32)
    weight = area[...]
    for start in range(0, CARRY, size):
        rows = slice(start, start + size)
        value = [
            payload_rows(stacks[k % 2], k // 2, start, size).astype(F32)
            for k in range(MEMBERS)
        ]
        slope = [jnp.zeros((size, ROWS), F32) for _ in range(MEMBERS)]
        pair = jnp.zeros((size, ROWS), F32)
        if start + size <= VARS:
            aim, share = target[rows, :], jnp.broadcast_to(weight, (size, ROWS))
        else:
            short = jnp.zeros((start + size - VARS, ROWS), F32)
            aim = jnp.concatenate([target[start:VARS, :], short], 0)
            share = jnp.where(iota((size, ROWS), 0) + start < VARS, weight, 0.0)
        for i in range(MEMBERS):
            for j in range(i + 1, MEMBERS):
                delta = value[i] - value[j]
                square = delta * delta + 0.0625
                root = lax.rsqrt(square)
                if i == 0:
                    pair = pair + square * root
                part = delta * root
                slope[i] = slope[i] + part
                slope[j] = slope[j] - part
        for i in range(MEMBERS):
            delta = value[i] - aim
            square = delta * delta + 0.0625
            root = lax.rsqrt(square)
            if i == 0:
                lost = lost + share * (square * root / MEMBERS - 0.5 * PAIR * pair)
            out = (share * (delta * root / MEMBERS - PAIR * slope[i])).astype(BF16)
            d_pred[rows, i * ROWS : (i + 1) * ROWS] = out
            if i == 0:
                d_own[rows, :] = out
    d_pred[CARRY:, :] = jnp.zeros((TILE - CARRY, MEMBERS * ROWS), BF16)
    d_own[CARRY:, :] = payload_rows(mine, 0, EDGE, 16)
    loss[...] = jnp.sum(lost, axis=(0, 1), keepdims=True) / (ROWS * SHARDS * VARS)


def backward_kernel(*refs):
    me = refs[0]
    sets = (refs[1:7], refs[7:13])
    (
        normal_tile, inverse, embed_turned, head_tile, head_sum, d_pred, loss, mine, theirs,
        payload, d_table, normed_all, d_mixed_all, d_score_all,
    ) = refs[13:]
    stacks = (mine, theirs)
    here = me[0]
    query = normal_tile[...]
    sums = head_sum[...]
    out = d_pred[...]
    wide = out.astype(F32)
    d_normed = dot(head_tile[...], out)
    levels = jnp.sum(wide * sums, 0, keepdims=True) / WIDTH
    for k in range(MEMBERS):
        side, i = k % 2, k // 2
        cols = slice(k * ROWS, (k + 1) * ROWS)
        mean, scale = stats_of(stacks[side], i)
        normed = (sets[side][5][i] - mean) * scale
        along = jnp.zeros((1, ROWS), F32)
        for start in range(0, VARS + NODES - VARS % NODES, NODES):
            pred = payload_rows(stacks[side], i, start, NODES).astype(F32)
            along = along + jnp.sum(pred * wide[start : start + NODES, cols], 0, keepdims=True)
        normed_all[:, cols] = normed.astype(BF16)
        d_mixed_all[:, cols] = (
            scale * (d_normed[:, cols] - levels[:, cols] - normed * (along / WIDTH))
        ).astype(BF16)
    d_head = dot_nt(normed_all[...], out)
    for k in range(MEMBERS):
        side, i = k % 2, k // 2
        rows = slice(i * BOTH, (i + 1) * BOTH)
        d_weight = dot(sets[side][4][rows, :], d_mixed_all[:, k * ROWS : (k + 1) * ROWS])
        weight = sets[side][1][rows, :].astype(F32).reshape(2, WIDE, ROWS)
        d_weight = d_weight.reshape(2, WIDE, ROWS)
        d_score = weight * (d_weight - jnp.sum(weight * d_weight, 1, keepdims=True))
        d_score_all[side, rows, :] = (
            (d_score * SIZE**-0.5).astype(BF16).reshape(BOTH, ROWS)
        )
    d_query = jnp.zeros((TILE, ROWS), F32)
    for side in range(2):
        turned, weights, keys, key_roots, values, hidden = sets[side]
        d_score = d_score_all[side]
        d_query = d_query + dot_tn(keys[...], d_score)
        d_both = dot_nt(d_score, query)
        parts = [slice(i * BOTH, (i + 1) * BOTH) for i in range(HALF)]
        d_key = jnp.concatenate([unstack_heads(d_both[rows]) for rows in parts], 0)
        key = jnp.concatenate([unstack_heads(keys[rows, :]) for rows in parts], 0).astype(F32)
        d_table[side, :, :TILE] = key_back(d_key, key, key_roots[...]).astype(BF16)
        for i, rows in enumerate(parts):
            k = 2 * i + side
            d_value = dot_nt(weights[rows, :], d_mixed_all[:, k * ROWS : (k + 1) * ROWS])
            d_table[side, i * WIDE : (i + 1) * WIDE, TILE:] = unstack_heads(d_value).astype(BF16)
    wide_query = query.astype(F32)
    along = d_query * wide_query
    along = jnp.concatenate(
        [
            jnp.broadcast_to(jnp.mean(along[:SIZE], 0, keepdims=True), (SIZE, ROWS)),
            jnp.broadcast_to(jnp.mean(along[SIZE:], 0, keepdims=True), (SIZE, ROWS)),
        ],
        0,
    )
    d_query = inverse[...] * (d_query - wide_query * along)
    grad = dot_nt(embed_turned[...], d_query.astype(BF16))
    payload[:, :TILE] = (grad * SCALE).astype(BF16)
    grad = dot(sets[0][0][...], d_table[0]) + dot(sets[1][0][...], d_table[1])
    payload[:, TILE : 3 * TILE] = (grad * SCALE).astype(BF16)
    high = loss[...].astype(BF16).astype(F32)
    lane = iota((WIDTH, TILE), 1)
    side = jnp.where(lane == VARS, high, jnp.where(lane == VARS + 1, loss[...] - high, 0.0))
    payload[:, 3 * TILE :] = side.astype(BF16)
    rows = pl.ds(pl.multiple_of(here * TILE, TILE), TILE)
    payload[rows, 3 * TILE :] = jnp.where(
        iota((TILE, TILE), 1) < VARS, d_head * SCALE, side[:TILE]
    ).astype(BF16)


def latent_kernel(
    d_own, weights, normed, table, normal, head, w_keyval,
    own, partner, other, d_table,
):
    tail = d_own[CARRY:, :].astype(F32)
    at = VARS + 2 - EDGE
    scale = tail[at : at + 1] + tail[at + 1 : at + 2]
    result = normed[...].astype(F32)
    d_normed = dot(head[...], d_own[...])
    level = jnp.mean(d_normed, 0, keepdims=True)
    along = jnp.mean(d_normed * result, 0, keepdims=True)
    d_mixed = (scale * (d_normed - level - result * along)).astype(BF16)
    for t in range(TILES):
        at = slice(t * TILE, (t + 1) * TILE)
        key, root = key_parts(table[:, at].astype(F32))
        value = table[:, WIDTH + t * TILE : WIDTH + (t + 1) * TILE]
        d_score, d_value, d_key = attention_back(
            weights[t], stack_heads(value), normal[at, :], d_mixed[at]
        )
        d_table[:, at] = key_back(d_key, key, root).astype(BF16)
        d_table[:, WIDTH + t * TILE : WIDTH + (t + 1) * TILE] = d_value.astype(BF16)
    total = dot_nt(d_table[...], w_keyval[...])
    own[...] = total[:NODES]
    partner[...] = total[NODES : 2 * NODES].astype(BF16)
    other[...] = total[2 * NODES :].astype(BF16)


def sum_kernel(me, pieces, stay, leave):
    low = jnp.sum(pieces[:, :NODES, :].astype(F32), 0)
    high = jnp.sum(pieces[:, NODES:, :].astype(F32), 0)
    even = jnp.bitwise_and(me[1], 1) == 0
    stay[...] = jnp.where(even, low, high)
    leave[...] = jnp.where(even, high, low).astype(BF16)


def merge_kernel(stay, came, total, loss):
    value = stay[...] + came[...].astype(F32)
    total[...] = value.astype(BF16)
    at = 3 * TILE + VARS
    loss[...] = value[0:1, at : at + 1] + value[0:1, at + 1 : at + 2]


def place_kernel(me, mine, theirs, latent, near, far, query, keyval, head, d_latent):
    here = me[0]
    total = jnp.zeros((NODES, TILE), F32)
    for k in range(MEMBERS):
        part = (mine, theirs)[k % 2][k // 2]
        at = pl.multiple_of(jnp.bitwise_xor(here, k) * TILE, TILE)
        query[:, pl.ds(at, TILE)] = part[:, :TILE].astype(F32)
        keyval[:, pl.ds(at, TILE)] = part[:, TILE : 2 * TILE].astype(F32)
        keyval[:, pl.ds(pl.multiple_of(WIDTH + at, TILE), TILE)] = part[
            :, 2 * TILE : 3 * TILE
        ].astype(F32)
        total = total + part[:, 3 * TILE :].astype(F32)
    head[...] = total[:, :VARS]
    d_latent[...] = latent[...] + near[...].astype(F32) + far[...].astype(F32)


def swap(array, axis, bits):
    count = lax.axis_size(axis)
    return lax.ppermute(array, axis, [(i, i ^ bits) for i in range(count)])


def beyond(array):
    step = lambda i: -1 if i % 2 == 0 else 1
    return lax.ppermute(array, "shard", [(i, (i + step(i)) % SHARDS) for i in range(SHARDS)])


def chips(array):
    return [array] + [swap(array, "member", k) for k in (2, 4, 6)]


def cores(*blocks):
    parts = [part for block in blocks for part in block]
    rows = sum(block[0].shape[0] for block in blocks)
    (mine,) = call(
        stack_kernel,
        [shape(HALF, rows, parts[0].shape[1])],
        [VMEM] * len(parts),
        size=1 << 20,
    )(*parts)
    return mine, swap(mine, "member", 1)


def shape(*dims, kind=BF16):
    return jax.ShapeDtypeStruct(dims, kind)


def on_device(latent, grid_embed, edge_src, area, target, w_query, w_keyval, w_head):
    member = lax.axis_index("member").astype(jnp.int32)
    shard = lax.axis_index("shard").astype(jnp.int32)
    me = jnp.stack([member, shard])
    own = latent[0]
    edges, head_turned = edge_src.T, w_head.T
    partner = swap(own, "shard", 1)
    other = beyond(own)
    own_far = chips(own)
    prepared = call(
        prepare_kernel,
        [
            shape(WIDTH, ROWS),
            shape(TILE, ROWS),
            shape(TILE, ROWS, kind=F32),
            shape(WIDTH, ROWS),
            shape(TILE, ROWS),
        ],
        [SMEM, VMEM, VMEM],
        flops=20 << 30,
        size=4 << 20,
    )(me, grid_embed, w_query)
    prepared, other, partner = lax.optimization_barrier((prepared, other, partner))
    normal, normal_tile, inverse, embed_turned, embed_tile = prepared
    partner_far = chips(partner)
    bundle, weights, normed, table = call(
        forward_kernel,
        [
            shape(2 * NODES, WIDTH),
            shape(TILES, BOTH, ROWS),
            shape(WIDTH, ROWS),
            shape(WIDE, 2 * WIDTH),
        ],
        [SMEM] + [VMEM] * 8,
        [pltpu.VMEM((WIDTH, ROWS), F32)],
    )(me, own, partner, other, w_keyval, normal, embed_turned, edges, head_turned)
    bundle, own_far = lax.optimization_barrier((bundle, own_far))
    stacks = cores(own_far, partner_far, chips(bundle))
    d_pred, d_own, loss = call(
        crps_kernel,
        [shape(TILE, MEMBERS * ROWS), shape(TILE, ROWS), shape(1, 1, kind=F32)],
        [VMEM] * 4,
    )(*stacks, target.T, area.reshape(1, ROWS))
    head, head_tile, head_sum = call(
        head_kernel,
        [shape(WIDTH, TILE), shape(TILE, TILE), shape(TILE, 1, kind=F32)],
        [SMEM, VMEM],
    )(me, head_turned)
    tables = [
        call(
            tables_kernel,
            [
                shape(WIDTH, HALF * WIDE),
                shape(HALF * BOTH, ROWS),
                shape(HALF * BOTH, TILE),
                shape(HALF * WIDE, TILE, kind=F32),
                shape(HALF * BOTH, TILE),
                shape(HALF, TILE, ROWS, kind=F32),
            ],
            [SMEM] + [VMEM] * 5,
            flops=1 << 30,
            size=4 << 20,
        )(me, stack, w_keyval, normal_tile, embed_tile, edges)
        for stack in stacks
    ]
    (grads,) = call(
        backward_kernel,
        [shape(WIDTH, 4 * TILE)],
        [SMEM] + [VMEM] * 21,
        [
            pltpu.VMEM((2, HALF * WIDE, 2 * TILE), BF16),
            pltpu.VMEM((TILE, MEMBERS * ROWS), BF16),
            pltpu.VMEM((TILE, MEMBERS * ROWS), BF16),
            pltpu.VMEM((2, HALF * BOTH, ROWS), BF16),
        ],
        flops=2 << 30,
        size=8 << 20,
    )(
        me, *tables[0], *tables[1], normal_tile, inverse, embed_turned, head_tile, head_sum,
        d_pred, loss, *stacks,
    )
    pieces = lax.all_to_all(
        grads.reshape(SHARDS // 2, 2 * NODES, 4 * TILE),
        "shard",
        0,
        0,
        axis_index_groups=[[2 * pair + side for pair in range(SHARDS // 2)] for side in range(2)],
    )
    mine, near, far = call(
        latent_kernel,
        [
            shape(NODES, WIDTH, kind=F32),
            shape(NODES, WIDTH),
            shape(NODES, WIDTH),
        ],
        [VMEM] * 7,
        [pltpu.VMEM((WIDE, 2 * WIDTH), BF16)],
        flops=16 << 30,
        size=8 << 20,
    )(d_own, weights, normed, table, normal, head, w_keyval)
    near = swap(near, "shard", 1)
    far = beyond(far)
    pieces, mine = lax.optimization_barrier((pieces, mine))
    stay, leave = call(
        sum_kernel,
        [shape(NODES, 4 * TILE, kind=F32), shape(NODES, 4 * TILE)],
        [SMEM, VMEM],
        flops=1 << 20,
        size=1 << 20,
    )(me, pieces)
    came = swap(leave, "shard", 1)
    came, near, far = lax.optimization_barrier((came, near, far))
    total, loss = call(
        merge_kernel,
        [shape(NODES, 4 * TILE), shape(1, 1, kind=F32)],
        [VMEM] * 2,
        flops=1 << 16,
        size=1 << 18,
    )(stay, came)
    parts = cores(chips(total))
    grad_query, grad_keyval, grad_head, d_latent = call(
        place_kernel,
        [
            shape(NODES, WIDTH, kind=F32),
            shape(NODES, 2 * WIDTH, kind=F32),
            shape(NODES, VARS, kind=F32),
            shape(NODES, WIDTH, kind=F32),
        ],
        [SMEM] + [VMEM] * 5,
        size=1 << 20,
    )(me, *parts, mine, near, far)
    return (loss.reshape(1), d_latent[None], grad_query, grad_keyval, grad_head)


def solution(mesh):
    placed = (
        P("member", "shard", None),
        P("shard", None),
        P("shard", None),
        P("shard"),
        P("shard", None),
        P(),
        P(),
        P(),
    )
    return jax.shard_map(
        on_device,
        mesh=mesh,
        in_specs=placed,
        out_specs=(
            P("member"),
            P("member", "shard", None),
            P("shard", None),
            P("shard", None),
            P("shard", None),
        ),
        check_vma=False,
    )
```

```python
import jax
import jax.numpy as jnp
from jax import lax
from jax.experimental import pallas as pl
from jax.experimental.pallas import tpu as pltpu
from jax.sharding import PartitionSpec as P

F32 = jnp.float32
BF16 = jnp.bfloat16
TILE = 128
SIZE = 64
TILES = 8
MEMBERS = 8
HALF = 4
SHARDS = 32
NODES = 32
WIDE = 96
BOTH = 2 * WIDE
ROWS = 256
WIDTH = 1024
VARS = 100
KNB = 3
CARRY = 112
EDGE = 96
FOLDS = 4
PAIR = 1.0 / (MEMBERS * (MEMBERS - 1))
SCALE = (MEMBERS * ROWS * SHARDS) ** (-0.5)
VMEM = pl.BlockSpec(memory_space=pltpu.VMEM)
SMEM = pl.BlockSpec(memory_space=pltpu.SMEM)


def dot(left, right):
    return lax.dot_general(left, right, (((1,), (0,)), ((), ())), preferred_element_type=F32)


def dot_nt(left, right):
    return lax.dot_general(left, right, (((1,), (1,)), ((), ())), preferred_element_type=F32)


def dot_tn(left, right):
    return lax.dot_general(left, right, (((0,), (0,)), ((), ())), preferred_element_type=F32)


def call(body, outs, specs, scratch=(), flops=0, size=0, limit=12):
    return pl.pallas_call(
        body,
        out_shape=outs,
        in_specs=specs,
        out_specs=[VMEM] * len(outs),
        scratch_shapes=list(scratch),
        compiler_params=pltpu.CompilerParams(vmem_limit_bytes=limit << 20),
        cost_estimate=pl.CostEstimate(flops=flops, bytes_accessed=size, transcendentals=0),
    )


def iota(shape, dim):
    return lax.broadcasted_iota(jnp.int32, shape, dim)


def lane_mean(values):
    average = jnp.where(
        iota((TILE, TILE), 0) // SIZE == iota((TILE, TILE), 1) // SIZE, 1.0 / SIZE, 0.0
    ).astype(BF16)
    high = values.astype(BF16)
    low = (values - high.astype(F32)).astype(BF16)
    return dot(high, average) + dot(low, average)


def stack_heads(tile):
    first = iota(tile.shape, 1) < SIZE
    zero = jnp.zeros_like(tile)
    return jnp.concatenate([jnp.where(first, tile, zero), jnp.where(first, zero, tile)], 0)


def unstack_heads(both):
    first = iota((WIDE, TILE), 1) < SIZE
    return jnp.where(first, both[:WIDE], both[WIDE:])


def half_sums(values):
    return (
        jnp.sum(values[:WIDE], 0, keepdims=True),
        jnp.sum(values[WIDE:], 0, keepdims=True),
    )


def key_parts(raw):
    root = lax.rsqrt(lane_mean(raw * raw) + 1e-06)
    return raw * root, root


def attention_back(weight, value, query, d_mixed):
    d_weight = dot(value, d_mixed)
    wide = weight.astype(F32)
    first, second = half_sums(wide * d_weight)
    d_score = jnp.concatenate([d_weight[:WIDE] - first, d_weight[WIDE:] - second], 0)
    d_score = (wide * d_score * SIZE**-0.5).astype(BF16)
    return d_score, unstack_heads(dot_nt(weight, d_mixed)), unstack_heads(dot_nt(d_score, query))


def key_back(d_key, normal, root):
    return root * (d_key - normal * lane_mean(d_key * normal))


def counts_of(edges, shard):
    source = edges[...]
    offset = jnp.bitwise_and(jnp.right_shift(source, 5) - shard + SHARDS, SHARDS - 1)
    toward = jnp.where(jnp.bitwise_and(shard, 1) == 0, 1, SHARDS - 1)
    slot = jnp.where(offset == 0, 0, jnp.where(offset == toward, 1, 2))
    index = slot * NODES + jnp.bitwise_and(source, NODES - 1)
    node = iota((WIDE, ROWS), 0)
    total = jnp.zeros((WIDE, ROWS), F32)
    for k in range(KNB):
        total = total + jnp.where(index[k : k + 1] == node, 1.0, 0.0)
    return total


def prepare_kernel(
    me, embed, w_query, normal, normal_tile, inverse, embed_turned, embed_tile
):
    here = me[0]
    at = pl.multiple_of(here * TILE, TILE)
    embed_turned[...] = embed[...].T
    embed_tile[...] = embed_turned[pl.ds(at, TILE), :]
    value = dot(embed[...], w_query[...]).T
    held = jnp.zeros((TILE, ROWS), F32)
    for t in range(TILES):
        roots = []
        for h in (2 * t, 2 * t + 1):
            part = value[h * SIZE : (h + 1) * SIZE]
            root = lax.rsqrt(jnp.mean(part * part, 0, keepdims=True) + 1e-06)
            normal[h * SIZE : (h + 1) * SIZE, :] = (part * root).astype(BF16)
            roots.append(jnp.broadcast_to(root, (SIZE, ROWS)))
        held = jnp.where(here == t, jnp.concatenate(roots, 0), held)
    inverse[...] = held
    normal_tile[...] = normal[pl.ds(at, TILE), :]


def weigh(scores, count):
    groups = scores.shape[0] // WIDE
    expon = jnp.exp(scores).reshape(groups, WIDE, ROWS) * count[None]
    weight = expon * (1.0 / jnp.sum(expon, 1, keepdims=True))
    return weight.astype(BF16).reshape(groups * WIDE, ROWS)


def forward_kernel(
    me, own, partner, other, w_keyval, normal, embed, edges, w_head,
    bundle, weights, normed, table, hidden,
):
    bundle[:NODES, :] = other[...]
    counts = counts_of(edges, me[1])
    wide = jnp.concatenate([own[...], partner[...], other[...]], 0)
    low = dot(wide, w_keyval[...]).astype(BF16)
    table[...] = low
    tiles = [slice(t * TILE, (t + 1) * TILE) for t in range(TILES)]
    raw = jnp.concatenate([low[:, at] for at in tiles], 0).astype(F32)
    keys = key_parts(raw)[0].astype(BF16) * BF16(SIZE**-0.5)
    scores = [
        dot(stack_heads(keys[t * WIDE : (t + 1) * WIDE]), normal[at, :])
        for t, at in enumerate(tiles)
    ]
    shares = [weigh(score, counts) for score in scores]
    for t, at in enumerate(tiles):
        weights[t] = shares[t]
        value = stack_heads(low[:, WIDTH + t * TILE : WIDTH + (t + 1) * TILE])
        hidden[at, :] = embed[at, :].astype(F32) + dot_tn(value, shares[t])
    whole = hidden[...]
    mean = jnp.mean(whole, 0, keepdims=True)
    center = whole - mean
    scale = lax.rsqrt(jnp.mean(center * center, 0, keepdims=True) + 1e-05)
    result = (center * scale).astype(BF16)
    normed[...] = result
    pred = dot(w_head[...], result)
    pred = jnp.concatenate([pred, jnp.zeros((TILE - VARS, ROWS), F32)], 0)
    row = iota(pred.shape, 0)
    for at, stat in ((VARS, mean), (VARS + 2, scale)):
        high = stat.astype(BF16).astype(F32)
        pred = jnp.where(row == at, high, pred)
        pred = jnp.where(row == at + 1, stat - high, pred)
    pred = pred.astype(BF16)
    for q in range(FOLDS):
        bundle[NODES:, q * ROWS : (q + 1) * ROWS] = pred[q * NODES : (q + 1) * NODES]


def stack_kernel(*refs):
    parts, out = refs[:-1], refs[-1]
    at = 0
    for b in range(len(parts) // HALF):
        rows = parts[b * HALF].shape[0]
        for i in range(HALF):
            out[i, at : at + rows, :] = parts[b * HALF + i][...]
        at += rows


def tables_kernel(
    me, stack, w_keyval, normal_tile, embed_tile, edges,
    turned, weights, keys, key_roots, values, hidden,
):
    at = pl.multiple_of(me[0] * TILE, TILE)
    flat = jnp.concatenate([stack[i, :WIDE, :] for i in range(HALF)], 0)
    turned[...] = flat.T
    key, root = key_parts(dot(flat, w_keyval[:, pl.ds(at, TILE)]).astype(BF16).astype(F32))
    at = pl.multiple_of(WIDTH + at, TILE)
    value = dot(flat, w_keyval[:, pl.ds(at, TILE)]).astype(BF16)
    key_roots[...] = root
    key = key.astype(BF16) * BF16(SIZE**-0.5)
    members = [slice(i * WIDE, (i + 1) * WIDE) for i in range(HALF)]
    key = jnp.concatenate([stack_heads(key[rows]) for rows in members], 0)
    value = jnp.concatenate([stack_heads(value[rows]) for rows in members], 0)
    keys[...] = key
    values[...] = value
    weight = weigh(dot(key, normal_tile[...]), counts_of(edges, me[1]))
    weights[...] = weight
    base = embed_tile[...].astype(F32)
    for i in range(HALF):
        rows = slice(i * BOTH, (i + 1) * BOTH)
        hidden[i] = base + dot_tn(value[rows], weight[rows])


def payload_rows(stack, i, start, size):
    fold, row = start // NODES, WIDE + start % NODES
    return stack[i, row : row + size, fold * ROWS : (fold + 1) * ROWS]


def stats_of(stack, i):
    rows = payload_rows(stack, i, EDGE, 16).astype(F32)
    at = VARS - EDGE
    mean = rows[at : at + 1] + rows[at + 1 : at + 2]
    return mean, rows[at + 2 : at + 3] + rows[at + 3 : at + 4]


def crps_kernel(mine, theirs, target, area, d_pred, d_own, loss):
    size = 16
    stacks = (mine, theirs)
    lost = jnp.zeros((size, ROWS), F32)
    weight = area[...]
    for start in range(0, CARRY, size):
        rows = slice(start, start + size)
        value = [
            payload_rows(stacks[k % 2], k // 2, start, size).astype(F32)
            for k in range(MEMBERS)
        ]
        slope = [jnp.zeros((size, ROWS), F32) for _ in range(MEMBERS)]
        pair = jnp.zeros((size, ROWS), F32)
        if start + size <= VARS:
            aim, share = target[rows, :], jnp.broadcast_to(weight, (size, ROWS))
        else:
            short = jnp.zeros((start + size - VARS, ROWS), F32)
            aim = jnp.concatenate([target[start:VARS, :], short], 0)
            share = jnp.where(iota((size, ROWS), 0) + start < VARS, weight, 0.0)
        for i in range(MEMBERS):
            for j in range(i + 1, MEMBERS):
                delta = value[i] - value[j]
                square = delta * delta + 0.0625
                root = lax.rsqrt(square)
                if i == 0:
                    pair = pair + square * root
                part = delta * root
                slope[i] = slope[i] + part
                slope[j] = slope[j] - part
        for i in range(MEMBERS):
            delta = value[i] - aim
            square = delta * delta + 0.0625
            root = lax.rsqrt(square)
            if i == 0:
                lost = lost + share * (square * root / MEMBERS - 0.5 * PAIR * pair)
            out = (share * (delta * root / MEMBERS - PAIR * slope[i])).astype(BF16)
            d_pred[rows, i * ROWS : (i + 1) * ROWS] = out
            if i == 0:
                d_own[rows, :] = out
    d_pred[CARRY:, :] = jnp.zeros((TILE - CARRY, MEMBERS * ROWS), BF16)
    d_own[CARRY:, :] = payload_rows(mine, 0, EDGE, 16)
    loss[...] = jnp.sum(lost, axis=(0, 1), keepdims=True) / (ROWS * SHARDS * VARS)


def backward_kernel(*refs):
    me = refs[0]
    sets = (refs[1:7], refs[7:13])
    (
        normal_tile, inverse, embed_turned, w_head, d_pred, loss, mine, theirs,
        payload, d_table, normed_all, d_mixed_all, d_score_all,
    ) = refs[13:]
    stacks = (mine, theirs)
    here = me[0]
    query = normal_tile[...]
    out = d_pred[...]
    wide = out.astype(F32)
    sums = jnp.sum(w_head[...].astype(F32), 1, keepdims=True)
    at = pl.multiple_of(here * TILE, TILE)
    d_normed = dot_tn(w_head[:, pl.ds(at, TILE)], out[:VARS])
    levels = jnp.sum(wide[:VARS] * sums, 0, keepdims=True) / WIDTH
    for k in range(MEMBERS):
        side, i = k % 2, k // 2
        cols = slice(k * ROWS, (k + 1) * ROWS)
        mean, scale = stats_of(stacks[side], i)
        normed = (sets[side][5][i] - mean) * scale
        along = jnp.zeros((1, ROWS), F32)
        for start in range(0, VARS + NODES - VARS % NODES, NODES):
            pred = payload_rows(stacks[side], i, start, NODES).astype(F32)
            along = along + jnp.sum(pred * wide[start : start + NODES, cols], 0, keepdims=True)
        normed_all[:, cols] = normed.astype(BF16)
        d_mixed_all[:, cols] = (
            scale * (d_normed[:, cols] - levels[:, cols] - normed * (along / WIDTH))
        ).astype(BF16)
    d_head = dot_nt(normed_all[...], out)
    for k in range(MEMBERS):
        side, i = k % 2, k // 2
        rows = slice(i * BOTH, (i + 1) * BOTH)
        d_weight = dot(sets[side][4][rows, :], d_mixed_all[:, k * ROWS : (k + 1) * ROWS])
        weight = sets[side][1][rows, :].astype(F32).reshape(2, WIDE, ROWS)
        d_weight = d_weight.reshape(2, WIDE, ROWS)
        d_score = weight * (d_weight - jnp.sum(weight * d_weight, 1, keepdims=True))
        d_score_all[side, rows, :] = d_score.astype(BF16).reshape(BOTH, ROWS)
    d_query = jnp.zeros((TILE, ROWS), F32)
    for side in range(2):
        turned, weights, keys, key_roots, values, hidden = sets[side]
        d_score = d_score_all[side]
        d_query = d_query + dot_tn(keys[...], d_score)
        d_both = dot_nt(d_score, query * BF16(SIZE**-0.5))
        parts = [slice(i * BOTH, (i + 1) * BOTH) for i in range(HALF)]
        d_key = jnp.concatenate([unstack_heads(d_both[rows]) for rows in parts], 0)
        key = jnp.concatenate([unstack_heads(keys[rows, :]) for rows in parts], 0)
        key = key.astype(F32) * SIZE**0.5
        d_table[side, :, :TILE] = key_back(d_key, key, key_roots[...] * SCALE).astype(BF16)
        for i, rows in enumerate(parts):
            k = 2 * i + side
            d_value = dot_nt(weights[rows, :], d_mixed_all[:, k * ROWS : (k + 1) * ROWS])
            d_table[side, i * WIDE : (i + 1) * WIDE, TILE:] = (
                unstack_heads(d_value) * SCALE
            ).astype(BF16)
    wide_query = query.astype(F32)
    along = d_query * wide_query
    along = jnp.concatenate(
        [
            jnp.broadcast_to(jnp.mean(along[:SIZE], 0, keepdims=True), (SIZE, ROWS)),
            jnp.broadcast_to(jnp.mean(along[SIZE:], 0, keepdims=True), (SIZE, ROWS)),
        ],
        0,
    )
    d_query = inverse[...] * SCALE * (d_query - wide_query * along)
    grad = dot_nt(embed_turned[...], d_query.astype(BF16))
    payload[:, :TILE] = grad.astype(BF16)
    grad = dot(sets[0][0][...], d_table[0]) + dot(sets[1][0][...], d_table[1])
    payload[:, TILE : 3 * TILE] = grad.astype(BF16)
    high = loss[...].astype(BF16).astype(F32)
    lane = iota((WIDTH, TILE), 1)
    side = jnp.where(lane == VARS, high, jnp.where(lane == VARS + 1, loss[...] - high, 0.0))
    payload[:, 3 * TILE :] = side.astype(BF16)
    rows = pl.ds(pl.multiple_of(here * TILE, TILE), TILE)
    payload[rows, 3 * TILE :] = jnp.where(
        iota((TILE, TILE), 1) < VARS, d_head * SCALE, side[:TILE]
    ).astype(BF16)


def latent_kernel(
    d_own, weights, normed, table, normal, w_head, w_keyval,
    own, partner, other, d_table,
):
    tail = d_own[CARRY:, :].astype(F32)
    at = VARS + 2 - EDGE
    scale = tail[at : at + 1] + tail[at + 1 : at + 2]
    result = normed[...].astype(F32)
    d_normed = dot_tn(w_head[...], d_own[:VARS, :])
    level = jnp.mean(d_normed, 0, keepdims=True)
    along = jnp.mean(d_normed * result, 0, keepdims=True)
    d_mixed = (scale * (d_normed - level - result * along)).astype(BF16)
    for t in range(TILES):
        at = slice(t * TILE, (t + 1) * TILE)
        key, root = key_parts(table[:, at].astype(F32))
        value = table[:, WIDTH + t * TILE : WIDTH + (t + 1) * TILE]
        d_score, d_value, d_key = attention_back(
            weights[t], stack_heads(value), normal[at, :], d_mixed[at]
        )
        d_table[:, at] = key_back(d_key, key, root).astype(BF16)
        d_table[:, WIDTH + t * TILE : WIDTH + (t + 1) * TILE] = d_value.astype(BF16)
    total = dot_nt(d_table[...], w_keyval[...])
    own[...] = total[:NODES]
    partner[...] = total[NODES : 2 * NODES].astype(BF16)
    other[...] = total[2 * NODES :].astype(BF16)


def sum_kernel(me, pieces, stay, leave):
    low = jnp.sum(pieces[:, :NODES, :].astype(F32), 0)
    high = jnp.sum(pieces[:, NODES:, :].astype(F32), 0)
    even = jnp.bitwise_and(me[1], 1) == 0
    stay[...] = jnp.where(even, low, high)
    leave[...] = jnp.where(even, high, low).astype(BF16)


def merge_kernel(stay, came, total, loss):
    value = stay[...] + came[...].astype(F32)
    total[...] = value.astype(BF16)
    at = 3 * TILE + VARS
    loss[...] = value[0:1, at : at + 1] + value[0:1, at + 1 : at + 2]


def place_kernel(me, mine, theirs, latent, near, far, query, keyval, head, d_latent):
    here = me[0]
    total = jnp.zeros((NODES, TILE), F32)
    for k in range(MEMBERS):
        part = (mine, theirs)[k % 2][k // 2]
        at = pl.multiple_of(jnp.bitwise_xor(here, k) * TILE, TILE)
        query[:, pl.ds(at, TILE)] = part[:, :TILE].astype(F32)
        keyval[:, pl.ds(at, TILE)] = part[:, TILE : 2 * TILE].astype(F32)
        keyval[:, pl.ds(pl.multiple_of(WIDTH + at, TILE), TILE)] = part[
            :, 2 * TILE : 3 * TILE
        ].astype(F32)
        total = total + part[:, 3 * TILE :].astype(F32)
    head[...] = total[:, :VARS]
    d_latent[...] = latent[...] + near[...].astype(F32) + far[...].astype(F32)


def swap(array, axis, bits):
    count = lax.axis_size(axis)
    return lax.ppermute(array, axis, [(i, i ^ bits) for i in range(count)])


def beyond(array):
    step = lambda i: -1 if i % 2 == 0 else 1
    return lax.ppermute(array, "shard", [(i, (i + step(i)) % SHARDS) for i in range(SHARDS)])


def chips(array):
    return [array] + [swap(array, "member", k) for k in (2, 4, 6)]


def cores(*blocks):
    parts = [part for block in blocks for part in block]
    rows = sum(block[0].shape[0] for block in blocks)
    (mine,) = call(
        stack_kernel,
        [shape(HALF, rows, parts[0].shape[1])],
        [VMEM] * len(parts),
        size=1 << 20,
    )(*parts)
    return mine, swap(mine, "member", 1)


def shape(*dims, kind=BF16):
    return jax.ShapeDtypeStruct(dims, kind)


def on_device(latent, grid_embed, edge_src, area, target, w_query, w_keyval, w_head):
    member = lax.axis_index("member").astype(jnp.int32)
    shard = lax.axis_index("shard").astype(jnp.int32)
    me = jnp.stack([member, shard])
    own = latent[0]
    edges, head_turned = edge_src.T, w_head.T
    partner = swap(own, "shard", 1)
    other = beyond(own)
    prepared = call(
        prepare_kernel,
        [
            shape(WIDTH, ROWS),
            shape(TILE, ROWS),
            shape(TILE, ROWS, kind=F32),
            shape(WIDTH, ROWS),
            shape(TILE, ROWS),
        ],
        [SMEM, VMEM, VMEM],
        flops=20 << 30,
        size=4 << 20,
    )(me, grid_embed, w_query)
    early, prepared = lax.optimization_barrier((own, prepared))
    own_far = chips(early)
    prepared, other, partner = lax.optimization_barrier((prepared, other, partner))
    normal, normal_tile, inverse, embed_turned, embed_tile = prepared
    partner_far = chips(partner)
    bundle, weights, normed, table = call(
        forward_kernel,
        [
            shape(2 * NODES, WIDTH),
            shape(TILES, BOTH, ROWS),
            shape(WIDTH, ROWS),
            shape(WIDE, 2 * WIDTH),
        ],
        [SMEM] + [VMEM] * 8,
        [pltpu.VMEM((WIDTH, ROWS), F32)],
    )(me, own, partner, other, w_keyval, normal, embed_turned, edges, head_turned)
    bundle, own_far = lax.optimization_barrier((bundle, own_far))
    stacks = cores(own_far, partner_far, chips(bundle))
    d_pred, d_own, loss = call(
        crps_kernel,
        [shape(TILE, MEMBERS * ROWS), shape(TILE, ROWS), shape(1, 1, kind=F32)],
        [VMEM] * 4,
    )(*stacks, target.T, area.reshape(1, ROWS))
    tables = [
        call(
            tables_kernel,
            [
                shape(WIDTH, HALF * WIDE),
                shape(HALF * BOTH, ROWS),
                shape(HALF * BOTH, TILE),
                shape(HALF * WIDE, TILE, kind=F32),
                shape(HALF * BOTH, TILE),
                shape(HALF, TILE, ROWS, kind=F32),
            ],
            [SMEM] + [VMEM] * 5,
            flops=1 << 30,
            size=4 << 20,
        )(me, stack, w_keyval, normal_tile, embed_tile, edges)
        for stack in stacks
    ]
    (grads,) = call(
        backward_kernel,
        [shape(WIDTH, 4 * TILE)],
        [SMEM] + [VMEM] * 20,
        [
            pltpu.VMEM((2, HALF * WIDE, 2 * TILE), BF16),
            pltpu.VMEM((TILE, MEMBERS * ROWS), BF16),
            pltpu.VMEM((TILE, MEMBERS * ROWS), BF16),
            pltpu.VMEM((2, HALF * BOTH, ROWS), BF16),
        ],
        flops=2 << 30,
        size=8 << 20,
    )(
        me, *tables[0], *tables[1], normal_tile, inverse, embed_turned, head_turned,
        d_pred, loss, *stacks,
    )
    pieces = lax.all_to_all(
        grads.reshape(SHARDS // 2, 2 * NODES, 4 * TILE),
        "shard",
        0,
        0,
        axis_index_groups=[[2 * pair + side for pair in range(SHARDS // 2)] for side in range(2)],
    )
    mine, near, far = call(
        latent_kernel,
        [
            shape(NODES, WIDTH, kind=F32),
            shape(NODES, WIDTH),
            shape(NODES, WIDTH),
        ],
        [VMEM] * 7,
        [pltpu.VMEM((WIDE, 2 * WIDTH), BF16)],
        flops=16 << 30,
        size=8 << 20,
    )(d_own, weights, normed, table, normal, head_turned, w_keyval)
    near = swap(near, "shard", 1)
    far = beyond(far)
    pieces, mine = lax.optimization_barrier((pieces, mine))
    stay, leave = call(
        sum_kernel,
        [shape(NODES, 4 * TILE, kind=F32), shape(NODES, 4 * TILE)],
        [SMEM, VMEM],
        flops=1 << 20,
        size=1 << 20,
    )(me, pieces)
    came = swap(leave, "shard", 1)
    came, near, far = lax.optimization_barrier((came, near, far))
    total, loss = call(
        merge_kernel,
        [shape(NODES, 4 * TILE), shape(1, 1, kind=F32)],
        [VMEM] * 2,
        flops=1 << 16,
        size=1 << 18,
    )(stay, came)
    parts = cores(chips(total))
    grad_query, grad_keyval, grad_head, d_latent = call(
        place_kernel,
        [
            shape(NODES, WIDTH, kind=F32),
            shape(NODES, 2 * WIDTH, kind=F32),
            shape(NODES, VARS, kind=F32),
            shape(NODES, WIDTH, kind=F32),
        ],
        [SMEM] + [VMEM] * 5,
        size=1 << 20,
    )(me, *parts, mine, near, far)
    return (loss.reshape(1), d_latent[None], grad_query, grad_keyval, grad_head)


def solution(mesh):
    placed = (
        P("member", "shard", None),
        P("shard", None),
        P("shard", None),
        P("shard"),
        P("shard", None),
        P(),
        P(),
        P(),
    )
    return jax.shard_map(
        on_device,
        mesh=mesh,
        in_specs=placed,
        out_specs=(
            P("member"),
            P("member", "shard", None),
            P("shard", None),
            P("shard", None),
            P("shard", None),
        ),
        check_vma=False,
    )
```

```python
import jax
import jax.numpy as jnp
from jax import lax
from jax.experimental import pallas as pl
from jax.experimental.pallas import tpu as pltpu
from jax.sharding import PartitionSpec as P

F32 = jnp.float32
BF16 = jnp.bfloat16
TILE = 128
SIZE = 64
TILES = 8
MEMBERS = 8
HALF = 4
SHARDS = 32
NODES = 32
WIDE = 96
BOTH = 2 * WIDE
ROWS = 256
WIDTH = 1024
VARS = 100
KNB = 3
PIECES = 4
CARRY = 112
EDGE = 96
FOLDS = 4
PAIR = 1.0 / (MEMBERS * (MEMBERS - 1))
SCALE = (MEMBERS * ROWS * SHARDS) ** (-0.5)
VMEM = pl.BlockSpec(memory_space=pltpu.VMEM)
SMEM = pl.BlockSpec(memory_space=pltpu.SMEM)


def dot(left, right):
    return lax.dot_general(left, right, (((1,), (0,)), ((), ())), preferred_element_type=F32)


def dot_nt(left, right):
    return lax.dot_general(left, right, (((1,), (1,)), ((), ())), preferred_element_type=F32)


def dot_tn(left, right):
    return lax.dot_general(left, right, (((0,), (0,)), ((), ())), preferred_element_type=F32)


def call(body, outs, specs, scratch=(), flops=0, size=0, limit=12, into=VMEM):
    return pl.pallas_call(
        body,
        out_shape=outs,
        in_specs=specs,
        out_specs=[into] * len(outs),
        scratch_shapes=list(scratch),
        compiler_params=pltpu.CompilerParams(vmem_limit_bytes=limit << 20),
        cost_estimate=pl.CostEstimate(flops=flops, bytes_accessed=size, transcendentals=0),
    )


def iota(shape, dim):
    return lax.broadcasted_iota(jnp.int32, shape, dim)


def lane_mean(values):
    average = jnp.where(
        iota((TILE, TILE), 0) // SIZE == iota((TILE, TILE), 1) // SIZE, 1.0 / SIZE, 0.0
    ).astype(BF16)
    return dot(values.astype(BF16), average)


def stack_heads(tile):
    first = iota(tile.shape, 1) < SIZE
    zero = jnp.zeros_like(tile)
    return jnp.concatenate([jnp.where(first, tile, zero), jnp.where(first, zero, tile)], 0)


def unstack_heads(both):
    first = iota((WIDE, TILE), 1) < SIZE
    return jnp.where(first, both[:WIDE], both[WIDE:])


def half_sums(values):
    return (
        jnp.sum(values[:WIDE], 0, keepdims=True),
        jnp.sum(values[WIDE:], 0, keepdims=True),
    )


def key_parts(raw):
    root = lax.rsqrt(lane_mean(raw * raw) + 1e-06)
    return raw * root, root


def attention_back(weight, value, query, d_mixed):
    d_weight = dot(value, d_mixed)
    wide = weight.astype(F32)
    first, second = half_sums(wide * d_weight)
    d_score = jnp.concatenate([d_weight[:WIDE] - first, d_weight[WIDE:] - second], 0)
    d_score = (wide * d_score * SIZE**-0.5).astype(BF16)
    return d_score, unstack_heads(dot_nt(weight, d_mixed)), unstack_heads(dot_nt(d_score, query))


def key_back(d_key, normal, root):
    return root * (d_key - normal * lane_mean(d_key * normal))


def counts_of(edges, shard):
    source = edges[...]
    offset = jnp.bitwise_and(jnp.right_shift(source, 5) - shard + SHARDS, SHARDS - 1)
    toward = jnp.where(jnp.bitwise_and(shard, 1) == 0, 1, SHARDS - 1)
    slot = jnp.where(offset == 0, 0, jnp.where(offset == toward, 1, 2))
    index = slot * NODES + jnp.bitwise_and(source, NODES - 1)
    node = iota((WIDE, ROWS), 0)
    total = jnp.zeros((WIDE, ROWS), F32)
    for k in range(KNB):
        total = total + jnp.where(index[k : k + 1] == node, 1.0, 0.0)
    return total


def prepare_kernel(
    me, embed, w_query, normal, normal_tile, inverse, embed_turned, embed_tile
):
    here = me[0]
    at = pl.multiple_of(here * TILE, TILE)
    embed_turned[...] = embed[...].T
    embed_tile[...] = embed_turned[pl.ds(at, TILE), :]
    value = dot(embed[...], w_query[...]).T
    held = jnp.zeros((TILE, ROWS), F32)
    for t in range(TILES):
        roots = []
        for h in (2 * t, 2 * t + 1):
            part = value[h * SIZE : (h + 1) * SIZE]
            root = lax.rsqrt(jnp.mean(part * part, 0, keepdims=True) + 1e-06)
            normal[h * SIZE : (h + 1) * SIZE, :] = (part * root).astype(BF16)
            roots.append(jnp.broadcast_to(root, (SIZE, ROWS)))
        held = jnp.where(here == t, jnp.concatenate(roots, 0), held)
    inverse[...] = held
    normal_tile[...] = normal[pl.ds(at, TILE), :]


def weigh(scores, count):
    groups = scores.shape[0] // WIDE
    expon = jnp.exp(scores).reshape(groups, WIDE, ROWS) * count[None]
    weight = expon * (1.0 / jnp.sum(expon, 1, keepdims=True))
    return weight.astype(BF16).reshape(groups * WIDE, ROWS)


def forward_kernel(
    me, own, partner, other, w_keyval, normal, embed, edges, w_head,
    bundle, weights, normed, table, hidden,
):
    bundle[:NODES, :] = other[...]
    counts = counts_of(edges, me[1])
    wide = jnp.concatenate([own[...], partner[...], other[...]], 0)
    low = dot(wide, w_keyval[...]).astype(BF16)
    table[...] = low
    tiles = [slice(t * TILE, (t + 1) * TILE) for t in range(TILES)]
    raw = jnp.concatenate([low[:, at] for at in tiles], 0).astype(F32)
    keys = key_parts(raw)[0].astype(BF16) * BF16(SIZE**-0.5)
    scores = [
        dot(stack_heads(keys[t * WIDE : (t + 1) * WIDE]), normal[at, :])
        for t, at in enumerate(tiles)
    ]
    shares = [weigh(score, counts) for score in scores]
    for t, at in enumerate(tiles):
        weights[t] = shares[t]
        value = stack_heads(low[:, WIDTH + t * TILE : WIDTH + (t + 1) * TILE])
        hidden[at, :] = embed[at, :].astype(F32) + dot_tn(value, shares[t])
    whole = hidden[...]
    mean = jnp.mean(whole, 0, keepdims=True)
    center = whole - mean
    scale = lax.rsqrt(jnp.mean(center * center, 0, keepdims=True) + 1e-05)
    result = (center * scale).astype(BF16)
    normed[...] = result
    pred = dot(w_head[...], result)
    pred = jnp.concatenate([pred, jnp.zeros((TILE - VARS, ROWS), F32)], 0)
    row = iota(pred.shape, 0)
    for at, stat in ((VARS, mean), (VARS + 2, scale)):
        high = stat.astype(BF16).astype(F32)
        pred = jnp.where(row == at, high, pred)
        pred = jnp.where(row == at + 1, stat - high, pred)
    pred = pred.astype(BF16)
    for q in range(FOLDS):
        bundle[NODES:, q * ROWS : (q + 1) * ROWS] = pred[q * NODES : (q + 1) * NODES]


def stack_kernel(*refs):
    parts, out = refs[:-1], refs[-1]
    at = 0
    for b in range(len(parts) // HALF):
        rows = parts[b * HALF].shape[0]
        for i in range(HALF):
            out[i, at : at + rows, :] = parts[b * HALF + i][...]
        at += rows


def tables_kernel(
    me, stack, w_keyval, normal_tile, embed_tile, edges,
    turned, weights, keys, key_roots, values, hidden,
):
    at = pl.multiple_of(me[0] * TILE, TILE)
    flat = jnp.concatenate([stack[i, :WIDE, :] for i in range(HALF)], 0)
    turned[...] = flat.T
    after = pl.multiple_of(WIDTH + at, TILE)
    tile = jnp.concatenate([w_keyval[:, pl.ds(at, TILE)], w_keyval[:, pl.ds(after, TILE)]], 1)
    table = dot(flat, tile).astype(BF16)
    key, root = key_parts(table[:, :TILE].astype(F32))
    value = table[:, TILE:]
    key_roots[...] = root
    key = key.astype(BF16) * BF16(SIZE**-0.5)
    members = [slice(i * WIDE, (i + 1) * WIDE) for i in range(HALF)]
    key = jnp.concatenate([stack_heads(key[rows]) for rows in members], 0)
    value = jnp.concatenate([stack_heads(value[rows]) for rows in members], 0)
    keys[...] = key
    values[...] = value
    weight = weigh(dot(key, normal_tile[...]), counts_of(edges, me[1]))
    weights[...] = weight
    base = embed_tile[...].astype(F32)
    for i in range(HALF):
        rows = slice(i * BOTH, (i + 1) * BOTH)
        hidden[i] = base + dot_tn(value[rows], weight[rows])


def payload_rows(stack, i, start, size):
    fold, row = start // NODES, WIDE + start % NODES
    return stack[i, row : row + size, fold * ROWS : (fold + 1) * ROWS]


def stats_of(stack, i):
    rows = payload_rows(stack, i, EDGE, 16).astype(F32)
    at = VARS - EDGE
    mean = rows[at : at + 1] + rows[at + 1 : at + 2]
    return mean, rows[at + 2 : at + 3] + rows[at + 3 : at + 4]


def crps_kernel(mine, theirs, target, area, w_head, d_pred, d_own, loss, sums):
    size = 16
    columns = jnp.sum(w_head[...].astype(F32), 1, keepdims=True) / WIDTH
    columns = jnp.concatenate([columns, jnp.zeros((CARRY - VARS, 1), F32)], 0)
    levels = [jnp.zeros((8, ROWS), F32) for _ in range(MEMBERS)]
    alongs = [jnp.zeros((8, ROWS), F32) for _ in range(MEMBERS)]
    stacks = (mine, theirs)
    lost = jnp.zeros((size, ROWS), F32)
    weight = area[...]
    for start in range(0, CARRY, size):
        rows = slice(start, start + size)
        value = [
            payload_rows(stacks[k % 2], k // 2, start, size).astype(F32)
            for k in range(MEMBERS)
        ]
        slope = [jnp.zeros((size, ROWS), F32) for _ in range(MEMBERS)]
        pair = jnp.zeros((size, ROWS), F32)
        if start + size <= VARS:
            aim, share = target[rows, :], jnp.broadcast_to(weight, (size, ROWS))
        else:
            short = jnp.zeros((start + size - VARS, ROWS), F32)
            aim = jnp.concatenate([target[start:VARS, :], short], 0)
            share = jnp.where(iota((size, ROWS), 0) + start < VARS, weight, 0.0)
        for i in range(MEMBERS):
            for j in range(i + 1, MEMBERS):
                delta = value[i] - value[j]
                square = delta * delta + 0.0625
                root = lax.rsqrt(square)
                if i == 0:
                    pair = pair + square * root
                part = delta * root
                slope[i] = slope[i] + part
                slope[j] = slope[j] - part
        for i in range(MEMBERS):
            delta = value[i] - aim
            square = delta * delta + 0.0625
            root = lax.rsqrt(square)
            if i == 0:
                lost = lost + share * (square * root / MEMBERS - 0.5 * PAIR * pair)
            wide = share * (delta * root / MEMBERS - PAIR * slope[i])
            part = wide * columns[rows]
            levels[i] = levels[i] + (part[:8] + part[8:])
            part = wide * value[i]
            alongs[i] = alongs[i] + (part[:8] + part[8:])
            out = wide.astype(BF16)
            d_pred[rows, i * ROWS : (i + 1) * ROWS] = out
            if i == 0:
                d_own[rows, :] = out
    for i in range(MEMBERS):
        sums[i : i + 1, :] = jnp.sum(levels[i], 0, keepdims=True)
        along = jnp.sum(alongs[i], 0, keepdims=True) / WIDTH
        sums[MEMBERS + i : MEMBERS + i + 1, :] = along
    d_pred[CARRY:, :] = jnp.zeros((TILE - CARRY, MEMBERS * ROWS), BF16)
    d_own[CARRY:, :] = payload_rows(mine, 0, EDGE, 16)
    loss[...] = jnp.sum(lost, axis=(0, 1), keepdims=True) / (ROWS * SHARDS * VARS)


def backward_kernel(*refs):
    me = refs[0]
    sets = (refs[1:7], refs[7:13])
    (
        normal_tile, inverse, embed_turned, w_head, d_pred, loss, sums, mine, theirs,
        payload_far, payload, sems, d_table, normed_all, d_mixed_all, d_score_all,
    ) = refs[13:]
    stacks = (mine, theirs)
    here = me[0]
    query = normal_tile[...]
    out = d_pred[...]
    at = pl.multiple_of(here * TILE, TILE)
    d_normed = dot_tn(w_head[:, pl.ds(at, TILE)], out[:VARS])
    for k in range(MEMBERS):
        side, i = k % 2, k // 2
        cols = slice(k * ROWS, (k + 1) * ROWS)
        mean, scale = stats_of(stacks[side], i)
        normed = (sets[side][5][i] - mean) * scale
        level, along = sums[k : k + 1, :], sums[MEMBERS + k : MEMBERS + k + 1, :]
        normed_all[:, cols] = normed.astype(BF16)
        d_mixed_all[:, cols] = (
            scale * (d_normed[:, cols] - level - normed * along)
        ).astype(BF16)
    d_head = dot_nt(normed_all[...], out)
    for k in range(MEMBERS):
        side, i = k % 2, k // 2
        rows = slice(i * BOTH, (i + 1) * BOTH)
        d_weight = dot(sets[side][4][rows, :], d_mixed_all[:, k * ROWS : (k + 1) * ROWS])
        weight = sets[side][1][rows, :].astype(F32).reshape(2, WIDE, ROWS)
        d_weight = d_weight.reshape(2, WIDE, ROWS)
        d_score = weight * (d_weight - jnp.sum(weight * d_weight, 1, keepdims=True))
        d_score_all[side, rows, :] = d_score.astype(BF16).reshape(BOTH, ROWS)
    d_query = jnp.zeros((TILE, ROWS), F32)
    for side in range(2):
        turned, weights, keys, key_roots, values, hidden = sets[side]
        d_score = d_score_all[side]
        d_query = d_query + dot_tn(keys[...], d_score)
        d_both = dot_nt(d_score, query * BF16(SIZE**-0.5))
        parts = [slice(i * BOTH, (i + 1) * BOTH) for i in range(HALF)]
        d_key = jnp.concatenate([unstack_heads(d_both[rows]) for rows in parts], 0)
        key = jnp.concatenate([unstack_heads(keys[rows, :]) for rows in parts], 0)
        key = key.astype(F32) * SIZE**0.5
        d_table[side, :, :TILE] = key_back(d_key, key, key_roots[...] * SCALE).astype(BF16)
        for i, rows in enumerate(parts):
            k = 2 * i + side
            d_value = dot_nt(weights[rows, :], d_mixed_all[:, k * ROWS : (k + 1) * ROWS])
            d_table[side, i * WIDE : (i + 1) * WIDE, TILE:] = (
                unstack_heads(d_value) * SCALE
            ).astype(BF16)
    wide_query = query.astype(F32)
    along = d_query * wide_query
    along = jnp.concatenate(
        [
            jnp.broadcast_to(jnp.mean(along[:SIZE], 0, keepdims=True), (SIZE, ROWS)),
            jnp.broadcast_to(jnp.mean(along[SIZE:], 0, keepdims=True), (SIZE, ROWS)),
        ],
        0,
    )
    d_query = inverse[...] * SCALE * (d_query - wide_query * along)
    payload[:, :TILE] = dot_nt(embed_turned[...], d_query.astype(BF16)).astype(BF16)
    high = loss[...].astype(BF16).astype(F32)
    lane = iota((WIDTH, TILE), 1)
    side = jnp.where(lane == VARS, high, jnp.where(lane == VARS + 1, loss[...] - high, 0.0))
    payload[:, 3 * TILE :] = side.astype(BF16)
    rows = pl.ds(pl.multiple_of(here * TILE, TILE), TILE)
    payload[rows, 3 * TILE :] = jnp.where(
        iota((TILE, TILE), 1) < VARS, d_head * SCALE, side[:TILE]
    ).astype(BF16)
    sent = []
    for step in range(PIECES):
        rows = slice(step * WIDTH // PIECES, (step + 1) * WIDTH // PIECES)
        grad = dot(sets[0][0][rows, :], d_table[0]) + dot(sets[1][0][rows, :], d_table[1])
        payload[rows, TILE : 3 * TILE] = grad.astype(BF16)
        sent.append(
            pltpu.make_async_copy(payload.at[rows, :], payload_far.at[rows, :], sems.at[step])
        )
        sent[-1].start()
    for copy in sent:
        copy.wait()


def latent_kernel(
    d_own, weights, normed, table, normal, w_head, w_keyval,
    own, partner, other, d_table,
):
    tail = d_own[CARRY:, :].astype(F32)
    at = VARS + 2 - EDGE
    scale = tail[at : at + 1] + tail[at + 1 : at + 2]
    result = normed[...].astype(F32)
    d_normed = dot_tn(w_head[...], d_own[:VARS, :])
    level = jnp.mean(d_normed, 0, keepdims=True)
    along = jnp.mean(d_normed * result, 0, keepdims=True)
    d_mixed = (scale * (d_normed - level - result * along)).astype(BF16)
    for t in range(TILES):
        at = slice(t * TILE, (t + 1) * TILE)
        key, root = key_parts(table[:, at].astype(F32))
        value = table[:, WIDTH + t * TILE : WIDTH + (t + 1) * TILE]
        d_score, d_value, d_key = attention_back(
            weights[t], stack_heads(value), normal[at, :], d_mixed[at]
        )
        d_table[:, at] = key_back(d_key, key, root).astype(BF16)
        d_table[:, WIDTH + t * TILE : WIDTH + (t + 1) * TILE] = d_value.astype(BF16)
    total = dot_nt(d_table[...], w_keyval[...])
    own[...] = total[:NODES]
    partner[...] = total[NODES : 2 * NODES].astype(BF16)
    other[...] = total[2 * NODES :].astype(BF16)


def sum_kernel(me, pieces, stay, leave):
    low = jnp.sum(pieces[:, :NODES, :].astype(F32), 0)
    high = jnp.sum(pieces[:, NODES:, :].astype(F32), 0)
    even = jnp.bitwise_and(me[1], 1) == 0
    stay[...] = jnp.where(even, low, high)
    leave[...] = jnp.where(even, high, low).astype(BF16)


def merge_kernel(stay, came, total, loss):
    value = stay[...] + came[...].astype(F32)
    total[...] = value.astype(BF16)
    at = 3 * TILE + VARS
    loss[...] = value[0:1, at : at + 1] + value[0:1, at + 1 : at + 2]


def place_kernel(me, mine, theirs, latent, near, far, query, keyval, head, d_latent):
    here = me[0]
    total = jnp.zeros((NODES, TILE), F32)
    for k in range(MEMBERS):
        part = (mine, theirs)[k % 2][k // 2]
        at = pl.multiple_of(jnp.bitwise_xor(here, k) * TILE, TILE)
        query[:, pl.ds(at, TILE)] = part[:, :TILE].astype(F32)
        keyval[:, pl.ds(at, TILE)] = part[:, TILE : 2 * TILE].astype(F32)
        keyval[:, pl.ds(pl.multiple_of(WIDTH + at, TILE), TILE)] = part[
            :, 2 * TILE : 3 * TILE
        ].astype(F32)
        total = total + part[:, 3 * TILE :].astype(F32)
    head[...] = total[:, :VARS]
    d_latent[...] = latent[...] + near[...].astype(F32) + far[...].astype(F32)


def swap(array, axis, bits):
    count = lax.axis_size(axis)
    return lax.ppermute(array, axis, [(i, i ^ bits) for i in range(count)])


def beyond(array):
    step = lambda i: -1 if i % 2 == 0 else 1
    return lax.ppermute(array, "shard", [(i, (i + step(i)) % SHARDS) for i in range(SHARDS)])


def chips(array):
    return [array] + [swap(array, "member", k) for k in (2, 4, 6)]


def cores(*blocks):
    parts = [part for block in blocks for part in block]
    rows = sum(block[0].shape[0] for block in blocks)
    (mine,) = call(
        stack_kernel,
        [shape(HALF, rows, parts[0].shape[1])],
        [VMEM] * len(parts),
        size=1 << 20,
    )(*parts)
    return mine, swap(mine, "member", 1)


def shape(*dims, kind=BF16):
    return jax.ShapeDtypeStruct(dims, kind)


def on_device(latent, grid_embed, edge_src, area, target, w_query, w_keyval, w_head):
    member = lax.axis_index("member").astype(jnp.int32)
    shard = lax.axis_index("shard").astype(jnp.int32)
    me = jnp.stack([member, shard])
    own = latent[0]
    edges, head_turned = edge_src.T, w_head.T
    partner = swap(own, "shard", 1)
    other = beyond(own)
    prepared = call(
        prepare_kernel,
        [
            shape(WIDTH, ROWS),
            shape(TILE, ROWS),
            shape(TILE, ROWS, kind=F32),
            shape(WIDTH, ROWS),
            shape(TILE, ROWS),
        ],
        [SMEM, VMEM, VMEM],
        flops=20 << 30,
        size=4 << 20,
    )(me, grid_embed, w_query)
    early, prepared = lax.optimization_barrier((own, prepared))
    own_far = chips(early)
    prepared, other, partner = lax.optimization_barrier((prepared, other, partner))
    normal, normal_tile, inverse, embed_turned, embed_tile = prepared
    partner_far = chips(partner)
    bundle, weights, normed, table = call(
        forward_kernel,
        [
            shape(2 * NODES, WIDTH),
            shape(TILES, BOTH, ROWS),
            shape(WIDTH, ROWS),
            shape(WIDE, 2 * WIDTH),
        ],
        [SMEM] + [VMEM] * 8,
        [pltpu.VMEM((WIDTH, ROWS), F32)],
    )(me, own, partner, other, w_keyval, normal, embed_turned, edges, head_turned)
    bundle, own_far = lax.optimization_barrier((bundle, own_far))
    stacks = cores(own_far, partner_far, chips(bundle))
    d_pred, d_own, loss, sums = call(
        crps_kernel,
        [
            shape(TILE, MEMBERS * ROWS),
            shape(TILE, ROWS),
            shape(1, 1, kind=F32),
            shape(2 * MEMBERS, ROWS, kind=F32),
        ],
        [VMEM] * 5,
    )(*stacks, target.T, area.reshape(1, ROWS), head_turned)
    tables = [
        call(
            tables_kernel,
            [
                shape(WIDTH, HALF * WIDE),
                shape(HALF * BOTH, ROWS),
                shape(HALF * BOTH, TILE),
                shape(HALF * WIDE, TILE, kind=F32),
                shape(HALF * BOTH, TILE),
                shape(HALF, TILE, ROWS, kind=F32),
            ],
            [SMEM] + [VMEM] * 5,
            flops=1 << 30,
            size=4 << 20,
        )(me, stack, w_keyval, normal_tile, embed_tile, edges)
        for stack in stacks
    ]
    (grads,) = call(
        backward_kernel,
        [shape(WIDTH, 4 * TILE)],
        [SMEM] + [VMEM] * 21,
        [
            pltpu.VMEM((WIDTH, 4 * TILE), BF16),
            pltpu.SemaphoreType.DMA((PIECES,)),
            pltpu.VMEM((2, HALF * WIDE, 2 * TILE), BF16),
            pltpu.VMEM((TILE, MEMBERS * ROWS), BF16),
            pltpu.VMEM((TILE, MEMBERS * ROWS), BF16),
            pltpu.VMEM((2, HALF * BOTH, ROWS), BF16),
        ],
        flops=2 << 30,
        size=8 << 20,
        into=pl.BlockSpec(memory_space=pl.ANY),
    )(
        me, *tables[0], *tables[1], normal_tile, inverse, embed_turned, head_turned,
        d_pred, loss, sums, *stacks,
    )
    pieces = lax.all_to_all(
        grads.reshape(SHARDS // 2, 2 * NODES, 4 * TILE),
        "shard",
        0,
        0,
        axis_index_groups=[[2 * pair + side for pair in range(SHARDS // 2)] for side in range(2)],
    )
    mine, near, far = call(
        latent_kernel,
        [
            shape(NODES, WIDTH, kind=F32),
            shape(NODES, WIDTH),
            shape(NODES, WIDTH),
        ],
        [VMEM] * 7,
        [pltpu.VMEM((WIDE, 2 * WIDTH), BF16)],
        flops=16 << 30,
        size=8 << 20,
    )(d_own, weights, normed, table, normal, head_turned, w_keyval)
    near = swap(near, "shard", 1)
    far = beyond(far)
    pieces, mine = lax.optimization_barrier((pieces, mine))
    stay, leave = call(
        sum_kernel,
        [shape(NODES, 4 * TILE, kind=F32), shape(NODES, 4 * TILE)],
        [SMEM, VMEM],
        flops=1 << 20,
        size=1 << 20,
    )(me, pieces)
    came = swap(leave, "shard", 1)
    came, near, far = lax.optimization_barrier((came, near, far))
    total, loss = call(
        merge_kernel,
        [shape(NODES, 4 * TILE), shape(1, 1, kind=F32)],
        [VMEM] * 2,
        flops=1 << 16,
        size=1 << 18,
    )(stay, came)
    parts = cores(chips(total))
    grad_query, grad_keyval, grad_head, d_latent = call(
        place_kernel,
        [
            shape(NODES, WIDTH, kind=F32),
            shape(NODES, 2 * WIDTH, kind=F32),
            shape(NODES, VARS, kind=F32),
            shape(NODES, WIDTH, kind=F32),
        ],
        [SMEM] + [VMEM] * 5,
        size=1 << 20,
    )(me, *parts, mine, near, far)
    return (loss.reshape(1), d_latent[None], grad_query, grad_keyval, grad_head)


def solution(mesh):
    placed = (
        P("member", "shard", None),
        P("shard", None),
        P("shard", None),
        P("shard"),
        P("shard", None),
        P(),
        P(),
        P(),
    )
    return jax.shard_map(
        on_device,
        mesh=mesh,
        in_specs=placed,
        out_specs=(
            P("member"),
            P("member", "shard", None),
            P("shard", None),
            P("shard", None),
            P("shard", None),
        ),
        check_vma=False,
    )
```

```python
import jax
import jax.numpy as jnp
from jax import lax
from jax.experimental import pallas as pl
from jax.experimental.pallas import tpu as pltpu
from jax.sharding import PartitionSpec as P

F32 = jnp.float32
BF16 = jnp.bfloat16
TILE = 128
SIZE = 64
TILES = 8
MEMBERS = 8
HALF = 4
SHARDS = 32
NODES = 32
WIDE = 96
BOTH = 2 * WIDE
ROWS = 256
WIDTH = 1024
VARS = 100
KNB = 3
PIECES = 4
CARRY = 112
EDGE = 96
FOLDS = 4
PAIR = 1.0 / (MEMBERS * (MEMBERS - 1))
SCALE = (MEMBERS * ROWS * SHARDS) ** (-0.5)
VMEM = pl.BlockSpec(memory_space=pltpu.VMEM)
SMEM = pl.BlockSpec(memory_space=pltpu.SMEM)


def dot(left, right):
    return lax.dot_general(left, right, (((1,), (0,)), ((), ())), preferred_element_type=F32)


def dot_nt(left, right):
    return lax.dot_general(left, right, (((1,), (1,)), ((), ())), preferred_element_type=F32)


def dot_tn(left, right):
    return lax.dot_general(left, right, (((0,), (0,)), ((), ())), preferred_element_type=F32)


def call(body, outs, specs, scratch=(), flops=0, size=0, limit=12, into=VMEM):
    return pl.pallas_call(
        body,
        out_shape=outs,
        in_specs=specs,
        out_specs=[into] * len(outs),
        scratch_shapes=list(scratch),
        compiler_params=pltpu.CompilerParams(vmem_limit_bytes=limit << 20),
        cost_estimate=pl.CostEstimate(flops=flops, bytes_accessed=size, transcendentals=0),
    )


def iota(shape, dim):
    return lax.broadcasted_iota(jnp.int32, shape, dim)


def lane_mean(values):
    average = jnp.where(
        iota((TILE, TILE), 0) // SIZE == iota((TILE, TILE), 1) // SIZE, 1.0 / SIZE, 0.0
    ).astype(BF16)
    return dot(values.astype(BF16), average)


def stack_heads(tile):
    first = iota(tile.shape, 1) < SIZE
    zero = jnp.zeros_like(tile)
    return jnp.concatenate([jnp.where(first, tile, zero), jnp.where(first, zero, tile)], 0)


def unstack_heads(both):
    first = iota((WIDE, TILE), 1) < SIZE
    return jnp.where(first, both[:WIDE], both[WIDE:])


def half_sums(values):
    return (
        jnp.sum(values[:WIDE], 0, keepdims=True),
        jnp.sum(values[WIDE:], 0, keepdims=True),
    )


def key_parts(raw):
    root = lax.rsqrt(lane_mean(raw * raw) + 1e-06)
    return raw * root, root


def attention_back(weight, value, query, d_mixed):
    d_weight = dot(value, d_mixed)
    wide = weight.astype(F32)
    first, second = half_sums(wide * d_weight)
    d_score = jnp.concatenate([d_weight[:WIDE] - first, d_weight[WIDE:] - second], 0)
    d_score = (wide * d_score * SIZE**-0.5).astype(BF16)
    return d_score, unstack_heads(dot_nt(weight, d_mixed)), unstack_heads(dot_nt(d_score, query))


def key_back(d_key, normal, root):
    return root * (d_key - normal * lane_mean(d_key * normal))


def counts_of(edges, shard):
    source = edges[...]
    offset = jnp.bitwise_and(jnp.right_shift(source, 5) - shard + SHARDS, SHARDS - 1)
    toward = jnp.where(jnp.bitwise_and(shard, 1) == 0, 1, SHARDS - 1)
    slot = jnp.where(offset == 0, 0, jnp.where(offset == toward, 1, 2))
    index = slot * NODES + jnp.bitwise_and(source, NODES - 1)
    node = iota((WIDE, ROWS), 0)
    total = jnp.zeros((WIDE, ROWS), F32)
    for k in range(KNB):
        total = total + jnp.where(index[k : k + 1] == node, 1.0, 0.0)
    return total


def prepare_kernel(
    me, embed, w_query, normal, normal_tile, inverse, embed_turned, embed_tile
):
    here = me[0]
    at = pl.multiple_of(here * TILE, TILE)
    embed_turned[...] = embed[...].T
    embed_tile[...] = embed_turned[pl.ds(at, TILE), :]
    value = dot(embed[...], w_query[...]).T
    held = jnp.zeros((TILE, ROWS), F32)
    for t in range(TILES):
        roots = []
        for h in (2 * t, 2 * t + 1):
            part = value[h * SIZE : (h + 1) * SIZE]
            root = lax.rsqrt(jnp.mean(part * part, 0, keepdims=True) + 1e-06)
            normal[h * SIZE : (h + 1) * SIZE, :] = (part * root).astype(BF16)
            roots.append(jnp.broadcast_to(root, (SIZE, ROWS)))
        held = jnp.where(here == t, jnp.concatenate(roots, 0), held)
    inverse[...] = held
    normal_tile[...] = normal[pl.ds(at, TILE), :]


def weigh(scores, count):
    groups = scores.shape[0] // WIDE
    expon = jnp.exp(scores).reshape(groups, WIDE, ROWS) * count[None]
    weight = expon * (1.0 / jnp.sum(expon, 1, keepdims=True))
    return weight.astype(BF16).reshape(groups * WIDE, ROWS)


def forward_kernel(
    me, own, partner, other, w_keyval, normal, embed, edges, w_head,
    bundle, weights, normed, table, hidden,
):
    bundle[:NODES, :] = other[...]
    counts = counts_of(edges, me[1])
    wide = jnp.concatenate([own[...], partner[...], other[...]], 0)
    low = dot(wide, w_keyval[...]).astype(BF16)
    table[...] = low
    tiles = [slice(t * TILE, (t + 1) * TILE) for t in range(TILES)]
    raw = jnp.concatenate([low[:, at] for at in tiles], 0).astype(F32)
    keys = key_parts(raw)[0].astype(BF16) * BF16(SIZE**-0.5)
    scores = [
        dot(stack_heads(keys[t * WIDE : (t + 1) * WIDE]), normal[at, :])
        for t, at in enumerate(tiles)
    ]
    shares = [weigh(score, counts) for score in scores]
    for t, at in enumerate(tiles):
        weights[t] = shares[t]
        value = stack_heads(low[:, WIDTH + t * TILE : WIDTH + (t + 1) * TILE])
        hidden[at, :] = embed[at, :].astype(F32) + dot_tn(value, shares[t])
    whole = hidden[...]
    mean = jnp.mean(whole, 0, keepdims=True)
    center = whole - mean
    scale = lax.rsqrt(jnp.mean(center * center, 0, keepdims=True) + 1e-05)
    result = (center * scale).astype(BF16)
    normed[...] = result
    pred = dot(w_head[...], result)
    pred = jnp.concatenate([pred, jnp.zeros((TILE - VARS, ROWS), F32)], 0)
    row = iota(pred.shape, 0)
    for at, stat in ((VARS, mean), (VARS + 2, scale)):
        high = stat.astype(BF16).astype(F32)
        pred = jnp.where(row == at, high, pred)
        pred = jnp.where(row == at + 1, stat - high, pred)
    pred = pred.astype(BF16)
    for q in range(FOLDS):
        bundle[NODES:, q * ROWS : (q + 1) * ROWS] = pred[q * NODES : (q + 1) * NODES]


def stack_kernel(*refs):
    parts, out = refs[:-1], refs[-1]
    at = 0
    for b in range(len(parts) // HALF):
        rows = parts[b * HALF].shape[0]
        for i in range(HALF):
            out[i, at : at + rows, :] = parts[b * HALF + i][...]
        at += rows


def tables_kernel(
    me, stack, w_keyval, normal_tile, embed_tile, edges,
    turned, weights, keys, key_roots, values, hidden,
):
    at = pl.multiple_of(me[0] * TILE, TILE)
    flat = jnp.concatenate([stack[i, :WIDE, :] for i in range(HALF)], 0)
    turned[...] = flat.T
    after = pl.multiple_of(WIDTH + at, TILE)
    tile = jnp.concatenate([w_keyval[:, pl.ds(at, TILE)], w_keyval[:, pl.ds(after, TILE)]], 1)
    table = dot(flat, tile).astype(BF16)
    key, root = key_parts(table[:, :TILE].astype(F32))
    value = table[:, TILE:]
    key_roots[...] = root
    key = key.astype(BF16) * BF16(SIZE**-0.5)
    members = [slice(i * WIDE, (i + 1) * WIDE) for i in range(HALF)]
    key = jnp.concatenate([stack_heads(key[rows]) for rows in members], 0)
    value = jnp.concatenate([stack_heads(value[rows]) for rows in members], 0)
    keys[...] = key
    values[...] = value
    weight = weigh(dot(key, normal_tile[...]), counts_of(edges, me[1]))
    weights[...] = weight
    base = embed_tile[...].astype(F32)
    for i in range(HALF):
        rows = slice(i * BOTH, (i + 1) * BOTH)
        hidden[i] = base + dot_tn(value[rows], weight[rows])


def payload_rows(stack, i, start, size):
    fold, row = start // NODES, WIDE + start % NODES
    return stack[i, row : row + size, fold * ROWS : (fold + 1) * ROWS]


def stats_of(stack, i):
    rows = payload_rows(stack, i, EDGE, 16).astype(F32)
    at = VARS - EDGE
    mean = rows[at : at + 1] + rows[at + 1 : at + 2]
    return mean, rows[at + 2 : at + 3] + rows[at + 3 : at + 4]


def crps_kernel(mine, theirs, target, area, w_head, d_pred, d_own, loss, sums):
    columns = jnp.sum(w_head[...].astype(F32), 1, keepdims=True) / WIDTH
    columns = jnp.concatenate([columns, jnp.zeros((CARRY - VARS, 1), F32)], 0)
    levels = [jnp.zeros((8, ROWS), F32) for _ in range(MEMBERS)]
    alongs = [jnp.zeros((8, ROWS), F32) for _ in range(MEMBERS)]
    stacks = (mine, theirs)
    lost = jnp.zeros((8, ROWS), F32)
    weight = area[...]
    fold = lambda part: part if part.shape[0] == 8 else part[:8] + part[8:]
    for start in range(0, CARRY, 16):
        size = min(16, VARS + 4 - start)
        rows = slice(start, start + size)
        value = [
            payload_rows(stacks[k % 2], k // 2, start, 16).astype(F32)[:size]
            for k in range(MEMBERS)
        ]
        slope = [jnp.zeros((size, ROWS), F32) for _ in range(MEMBERS)]
        pair = jnp.zeros((size, ROWS), F32)
        if start + size <= VARS:
            aim, share = target[rows, :], jnp.broadcast_to(weight, (size, ROWS))
        else:
            short = jnp.zeros((start + size - VARS, ROWS), F32)
            aim = jnp.concatenate([target[start:VARS, :], short], 0)
            share = jnp.where(iota((size, ROWS), 0) + start < VARS, weight, 0.0)
        for i in range(MEMBERS):
            for j in range(i + 1, MEMBERS):
                delta = value[i] - value[j]
                square = delta * delta + 0.0625
                root = lax.rsqrt(square)
                if i == 0:
                    pair = pair + square * root
                part = delta * root
                slope[i] = slope[i] + part
                slope[j] = slope[j] - part
        for i in range(MEMBERS):
            delta = value[i] - aim
            square = delta * delta + 0.0625
            root = lax.rsqrt(square)
            if i == 0:
                lost = lost + fold(share * (square * root / MEMBERS - 0.5 * PAIR * pair))
            wide = share * (delta * root / MEMBERS - PAIR * slope[i])
            part = wide * columns[start : start + size]
            levels[i] = levels[i] + fold(part)
            part = wide * value[i]
            alongs[i] = alongs[i] + fold(part)
            if size < 16:
                wide = jnp.concatenate([wide, jnp.zeros((16 - size, ROWS), F32)], 0)
            out = wide.astype(BF16)
            rows = slice(start, start + 16)
            d_pred[rows, i * ROWS : (i + 1) * ROWS] = out
            if i == 0:
                d_own[rows, :] = out
    for i in range(MEMBERS):
        sums[i : i + 1, :] = jnp.sum(levels[i], 0, keepdims=True)
        along = jnp.sum(alongs[i], 0, keepdims=True) / WIDTH
        sums[MEMBERS + i : MEMBERS + i + 1, :] = along
    d_pred[CARRY:, :] = jnp.zeros((TILE - CARRY, MEMBERS * ROWS), BF16)
    d_own[CARRY:, :] = payload_rows(mine, 0, EDGE, 16)
    loss[...] = jnp.sum(lost, axis=(0, 1), keepdims=True) / (ROWS * SHARDS * VARS)


def backward_kernel(*refs):
    me = refs[0]
    sets = (refs[1:7], refs[7:13])
    (
        normal_tile, inverse, embed_turned, w_head, d_pred, loss, sums, mine, theirs,
        payload_far, payload, sems, d_table, normed_all, d_mixed_all, d_score_all,
    ) = refs[13:]
    stacks = (mine, theirs)
    here = me[0]
    query = normal_tile[...]
    out = d_pred[...]
    at = pl.multiple_of(here * TILE, TILE)
    d_normed = dot_tn(w_head[:, pl.ds(at, TILE)], out[:VARS])
    for k in range(MEMBERS):
        side, i = k % 2, k // 2
        cols = slice(k * ROWS, (k + 1) * ROWS)
        mean, scale = stats_of(stacks[side], i)
        normed = (sets[side][5][i] - mean) * scale
        level, along = sums[k : k + 1, :], sums[MEMBERS + k : MEMBERS + k + 1, :]
        normed_all[:, cols] = normed.astype(BF16)
        d_mixed_all[:, cols] = (
            scale * (d_normed[:, cols] - level - normed * along)
        ).astype(BF16)
    d_head = dot_nt(normed_all[...], out)
    for k in range(MEMBERS):
        side, i = k % 2, k // 2
        rows = slice(i * BOTH, (i + 1) * BOTH)
        d_weight = dot(sets[side][4][rows, :], d_mixed_all[:, k * ROWS : (k + 1) * ROWS])
        weight = sets[side][1][rows, :].astype(F32).reshape(2, WIDE, ROWS)
        d_weight = d_weight.reshape(2, WIDE, ROWS)
        d_score = weight * (d_weight - jnp.sum(weight * d_weight, 1, keepdims=True))
        d_score_all[side, rows, :] = d_score.astype(BF16).reshape(BOTH, ROWS)
    d_query = jnp.zeros((TILE, ROWS), F32)
    for side in range(2):
        turned, weights, keys, key_roots, values, hidden = sets[side]
        d_score = d_score_all[side]
        d_query = d_query + dot_tn(keys[...], d_score)
        d_both = dot_nt(d_score, query * BF16(SIZE**-0.5))
        parts = [slice(i * BOTH, (i + 1) * BOTH) for i in range(HALF)]
        d_key = jnp.concatenate([unstack_heads(d_both[rows]) for rows in parts], 0)
        key = jnp.concatenate([unstack_heads(keys[rows, :]) for rows in parts], 0)
        key = key.astype(F32) * SIZE**0.5
        d_table[side, :, :TILE] = key_back(d_key, key, key_roots[...] * SCALE).astype(BF16)
        for i, rows in enumerate(parts):
            k = 2 * i + side
            d_value = dot_nt(weights[rows, :], d_mixed_all[:, k * ROWS : (k + 1) * ROWS])
            d_table[side, i * WIDE : (i + 1) * WIDE, TILE:] = (
                unstack_heads(d_value) * SCALE
            ).astype(BF16)
    wide_query = query.astype(F32)
    along = d_query * wide_query
    along = jnp.concatenate(
        [
            jnp.broadcast_to(jnp.mean(along[:SIZE], 0, keepdims=True), (SIZE, ROWS)),
            jnp.broadcast_to(jnp.mean(along[SIZE:], 0, keepdims=True), (SIZE, ROWS)),
        ],
        0,
    )
    d_query = inverse[...] * SCALE * (d_query - wide_query * along)
    payload[:, :TILE] = dot_nt(embed_turned[...], d_query.astype(BF16)).astype(BF16)
    high = loss[...].astype(BF16).astype(F32)
    lane = iota((WIDTH, TILE), 1)
    side = jnp.where(lane == VARS, high, jnp.where(lane == VARS + 1, loss[...] - high, 0.0))
    payload[:, 3 * TILE :] = side.astype(BF16)
    rows = pl.ds(pl.multiple_of(here * TILE, TILE), TILE)
    payload[rows, 3 * TILE :] = jnp.where(
        iota((TILE, TILE), 1) < VARS, d_head * SCALE, side[:TILE]
    ).astype(BF16)
    sent = []
    for step in range(PIECES):
        rows = slice(step * WIDTH // PIECES, (step + 1) * WIDTH // PIECES)
        grad = dot(sets[0][0][rows, :], d_table[0]) + dot(sets[1][0][rows, :], d_table[1])
        payload[rows, TILE : 3 * TILE] = grad.astype(BF16)
        sent.append(
            pltpu.make_async_copy(payload.at[rows, :], payload_far.at[rows, :], sems.at[step])
        )
        sent[-1].start()
    for copy in sent:
        copy.wait()


def latent_kernel(
    d_own, weights, normed, table, normal, w_head, w_keyval,
    own, partner, other, d_table,
):
    tail = d_own[CARRY:, :].astype(F32)
    at = VARS + 2 - EDGE
    scale = tail[at : at + 1] + tail[at + 1 : at + 2]
    result = normed[...].astype(F32)
    d_normed = dot_tn(w_head[...], d_own[:VARS, :])
    level = jnp.mean(d_normed, 0, keepdims=True)
    along = jnp.mean(d_normed * result, 0, keepdims=True)
    d_mixed = (scale * (d_normed - level - result * along)).astype(BF16)
    for t in range(TILES):
        at = slice(t * TILE, (t + 1) * TILE)
        key, root = key_parts(table[:, at].astype(F32))
        value = table[:, WIDTH + t * TILE : WIDTH + (t + 1) * TILE]
        d_score, d_value, d_key = attention_back(
            weights[t], stack_heads(value), normal[at, :], d_mixed[at]
        )
        d_table[:, at] = key_back(d_key, key, root).astype(BF16)
        d_table[:, WIDTH + t * TILE : WIDTH + (t + 1) * TILE] = d_value.astype(BF16)
    total = dot_nt(d_table[...], w_keyval[...])
    own[...] = total[:NODES]
    partner[...] = total[NODES : 2 * NODES].astype(BF16)
    other[...] = total[2 * NODES :].astype(BF16)


def sum_kernel(me, pieces, stay, leave):
    low = jnp.sum(pieces[:, :NODES, :].astype(F32), 0)
    high = jnp.sum(pieces[:, NODES:, :].astype(F32), 0)
    even = jnp.bitwise_and(me[1], 1) == 0
    stay[...] = jnp.where(even, low, high)
    leave[...] = jnp.where(even, high, low).astype(BF16)


def merge_kernel(stay, came, total, loss):
    value = stay[...] + came[...].astype(F32)
    total[...] = value.astype(BF16)
    at = 3 * TILE + VARS
    loss[...] = value[0:1, at : at + 1] + value[0:1, at + 1 : at + 2]


def place_kernel(me, mine, theirs, query, keyval, head):
    here = me[0]
    total = jnp.zeros((NODES, TILE), F32)
    for k in range(MEMBERS):
        part = (mine, theirs)[k % 2][k // 2]
        at = pl.multiple_of(jnp.bitwise_xor(here, k) * TILE, TILE)
        query[:, pl.ds(at, TILE)] = part[:, :TILE].astype(F32)
        keyval[:, pl.ds(at, TILE)] = part[:, TILE : 2 * TILE].astype(F32)
        keyval[:, pl.ds(pl.multiple_of(WIDTH + at, TILE), TILE)] = part[
            :, 2 * TILE : 3 * TILE
        ].astype(F32)
        total = total + part[:, 3 * TILE :].astype(F32)
    head[...] = total[:, :VARS]


def gather_kernel(latent, near, far, d_latent):
    d_latent[...] = latent[...] + near[...].astype(F32) + far[...].astype(F32)


def swap(array, axis, bits):
    count = lax.axis_size(axis)
    return lax.ppermute(array, axis, [(i, i ^ bits) for i in range(count)])


def beyond(array):
    step = lambda i: -1 if i % 2 == 0 else 1
    return lax.ppermute(array, "shard", [(i, (i + step(i)) % SHARDS) for i in range(SHARDS)])


def chips(array):
    return [array] + [swap(array, "member", k) for k in (2, 4, 6)]


def cores(*blocks):
    parts = [part for block in blocks for part in block]
    rows = sum(block[0].shape[0] for block in blocks)
    (mine,) = call(
        stack_kernel,
        [shape(HALF, rows, parts[0].shape[1])],
        [VMEM] * len(parts),
        size=1 << 20,
    )(*parts)
    return mine, swap(mine, "member", 1)


def shape(*dims, kind=BF16):
    return jax.ShapeDtypeStruct(dims, kind)


def on_device(latent, grid_embed, edge_src, area, target, w_query, w_keyval, w_head):
    member = lax.axis_index("member").astype(jnp.int32)
    shard = lax.axis_index("shard").astype(jnp.int32)
    me = jnp.stack([member, shard])
    own = latent[0]
    edges, head_turned = edge_src.T, w_head.T
    partner = swap(own, "shard", 1)
    other = beyond(own)
    prepared = call(
        prepare_kernel,
        [
            shape(WIDTH, ROWS),
            shape(TILE, ROWS),
            shape(TILE, ROWS, kind=F32),
            shape(WIDTH, ROWS),
            shape(TILE, ROWS),
        ],
        [SMEM, VMEM, VMEM],
        flops=20 << 30,
        size=4 << 20,
    )(me, grid_embed, w_query)
    early, prepared = lax.optimization_barrier((own, prepared))
    own_far = chips(early)
    prepared, other, partner = lax.optimization_barrier((prepared, other, partner))
    normal, normal_tile, inverse, embed_turned, embed_tile = prepared
    partner_far = chips(partner)
    bundle, weights, normed, table = call(
        forward_kernel,
        [
            shape(2 * NODES, WIDTH),
            shape(TILES, BOTH, ROWS),
            shape(WIDTH, ROWS),
            shape(WIDE, 2 * WIDTH),
        ],
        [SMEM] + [VMEM] * 8,
        [pltpu.VMEM((WIDTH, ROWS), F32)],
    )(me, own, partner, other, w_keyval, normal, embed_turned, edges, head_turned)
    bundle, own_far = lax.optimization_barrier((bundle, own_far))
    stacks = cores(own_far, partner_far, chips(bundle))
    d_pred, d_own, loss, sums = call(
        crps_kernel,
        [
            shape(TILE, MEMBERS * ROWS),
            shape(TILE, ROWS),
            shape(1, 1, kind=F32),
            shape(2 * MEMBERS, ROWS, kind=F32),
        ],
        [VMEM] * 5,
    )(*stacks, target.T, area.reshape(1, ROWS), head_turned)
    tables = [
        call(
            tables_kernel,
            [
                shape(WIDTH, HALF * WIDE),
                shape(HALF * BOTH, ROWS),
                shape(HALF * BOTH, TILE),
                shape(HALF * WIDE, TILE, kind=F32),
                shape(HALF * BOTH, TILE),
                shape(HALF, TILE, ROWS, kind=F32),
            ],
            [SMEM] + [VMEM] * 5,
            flops=1 << 30,
            size=4 << 20,
        )(me, stack, w_keyval, normal_tile, embed_tile, edges)
        for stack in stacks
    ]
    (grads,) = call(
        backward_kernel,
        [shape(WIDTH, 4 * TILE)],
        [SMEM] + [VMEM] * 21,
        [
            pltpu.VMEM((WIDTH, 4 * TILE), BF16),
            pltpu.SemaphoreType.DMA((PIECES,)),
            pltpu.VMEM((2, HALF * WIDE, 2 * TILE), BF16),
            pltpu.VMEM((TILE, MEMBERS * ROWS), BF16),
            pltpu.VMEM((TILE, MEMBERS * ROWS), BF16),
            pltpu.VMEM((2, HALF * BOTH, ROWS), BF16),
        ],
        flops=2 << 30,
        size=8 << 20,
        into=pl.BlockSpec(memory_space=pl.ANY),
    )(
        me, *tables[0], *tables[1], normal_tile, inverse, embed_turned, head_turned,
        d_pred, loss, sums, *stacks,
    )
    pieces = lax.all_to_all(
        grads.reshape(SHARDS // 2, 2 * NODES, 4 * TILE),
        "shard",
        0,
        0,
        axis_index_groups=[[2 * pair + side for pair in range(SHARDS // 2)] for side in range(2)],
    )
    mine, near, far = call(
        latent_kernel,
        [
            shape(NODES, WIDTH, kind=F32),
            shape(NODES, WIDTH),
            shape(NODES, WIDTH),
        ],
        [VMEM] * 7,
        [pltpu.VMEM((WIDE, 2 * WIDTH), BF16)],
        flops=16 << 30,
        size=8 << 20,
    )(d_own, weights, normed, table, normal, head_turned, w_keyval)
    near = swap(near, "shard", 1)
    far = beyond(far)
    pieces, mine = lax.optimization_barrier((pieces, mine))
    stay, leave = call(
        sum_kernel,
        [shape(NODES, 4 * TILE, kind=F32), shape(NODES, 4 * TILE)],
        [SMEM, VMEM],
        flops=1 << 20,
        size=1 << 20,
    )(me, pieces)
    came = swap(leave, "shard", 1)
    came, near, far = lax.optimization_barrier((came, near, far))
    total, loss = call(
        merge_kernel,
        [shape(NODES, 4 * TILE), shape(1, 1, kind=F32)],
        [VMEM] * 2,
        flops=1 << 16,
        size=1 << 18,
    )(stay, came)
    parts = cores(chips(total))
    (d_latent,) = call(gather_kernel, [shape(NODES, WIDTH, kind=F32)], [VMEM] * 3)(
        mine, near, far
    )
    grad_query, grad_keyval, grad_head = call(
        place_kernel,
        [
            shape(NODES, WIDTH, kind=F32),
            shape(NODES, 2 * WIDTH, kind=F32),
            shape(NODES, VARS, kind=F32),
        ],
        [SMEM] + [VMEM] * 2,
        size=1 << 20,
    )(me, *parts)
    return (loss.reshape(1), d_latent[None], grad_query, grad_keyval, grad_head)


def solution(mesh):
    placed = (
        P("member", "shard", None),
        P("shard", None),
        P("shard", None),
        P("shard"),
        P("shard", None),
        P(),
        P(),
        P(),
    )
    return jax.shard_map(
        on_device,
        mesh=mesh,
        in_specs=placed,
        out_specs=(
            P("member"),
            P("member", "shard", None),
            P("shard", None),
            P("shard", None),
            P("shard", None),
        ),
        check_vma=False,
    )
```
